256 devices in a mesh: lat: 16 (over y_hi, x, core), lon: 16 (over y_lo, z).
Axes of the slice: x: 4, y: 4 (y_hi: 2, y_lo: 2; y = y_hi * 2 + y_lo), z: 8, core: 2. Of those that a mesh axis runs over, the one named last changes fastest.
Arguments:
- grid_features: bfloat16 [32, 2048, 512], P('lat', 'lon'), may hold values from -18 to 18
- widths: int32 [32], replicated, may hold values from 32 to 1024, as said below
- w_query: bfloat16 [512, 512], replicated, may hold values from -1 to 1
- w_keyval: bfloat16 [1536, 1024], replicated, may hold values from -1 to 1
- w_out: bfloat16 [512, 512], replicated, may hold values from -0.25 to 0.25
Outputs:
- layer_out: bfloat16 [32, 2048, 512], P('lat', 'lon')
The draws below stay inside these ranges and needn't reach their ends.
Inputs may be any that keep to these rules, and one draw needn't show every extreme that they name: `widths`: rows 0 and 31 hold 2048 // 2 (their neighborhood is the whole longitude circle); every other row holds a value from 32 to 128, and some such row holds exactly 128.
All inputs are finite; a program needn't handle non-finite values.
Results may differ from the reference program's by a relative error of at most 0.0085.
Values may be sent and summed in bfloat16 or wider, within the bound.
No kernel may reach another device: no remote copies, remote signals or barrier semaphores. Data moves between devices by JAX's collectives and lax.ppermute only.
A program may use at most 128 MiB of HBM per device.

```python
import math
import jax
import jax.numpy as jnp
from jax import lax

HEADS = 8
HDIM = 64
C = 512
LON_DEV = 128
NLAT = 32
NLON = 2048
N_LON = 16


def shared_basis(key):
    return jnp.clip(jax.random.normal(key, (C, C), jnp.float32), -4.0, 4.0)


def draw_widths(key, part):
    key = jax.random.fold_in(key, 7)
    first_key, second_key = jax.random.split(key)
    inner_rows = jax.random.randint(first_key, (NLAT,), LON_DEV // 4, LON_DEV + 1)
    chosen = jax.random.randint(second_key, (), 1, NLAT - 1)
    row_ids = jnp.arange(NLAT)
    inner_rows = jnp.where(row_ids == chosen, LON_DEV, inner_rows)
    polar = (row_ids == 0) | (row_ids == NLAT - 1)
    return jnp.where(polar, NLON // 2, inner_rows).astype(jnp.int32)


def draw_w_query(key, part):
    basis = shared_basis(key)
    return jnp.clip(basis * C ** (-0.5), -1.0, 1.0).astype(jnp.bfloat16)


def draw_w_keyval(key, part):
    key = jax.random.fold_in(key, 13)
    fan_scale = (3 * C) ** (-0.5)
    fresh = jnp.clip(jax.random.normal(key, (3 * C, 2 * C), jnp.float32), -4.0, 4.0)
    weight = fresh * fan_scale
    return jnp.clip(weight, -1.0, 1.0).astype(jnp.bfloat16)


def draw_grid_features(key, part):
    key = jax.random.fold_in(key, 5)
    base_key = jax.random.fold_in(key, 0)
    shape = (NLAT, NLON, C)
    return jnp.clip(jax.random.normal(base_key, shape, jnp.float32), -6.0, 6.0).astype(jnp.bfloat16)


def scatter_about(key, shape, scale, bound, kind=jnp.bfloat16):
    drawn = jax.random.normal(key, shape, jnp.float32) * scale
    return jnp.minimum(jnp.maximum(drawn, -bound), bound).astype(kind)


def setup_inputs(seed: int = 0) -> dict:
    key_of = jax.random.split(jax.random.key(seed), 6)
    return {
        "grid_features": draw_grid_features(jax.random.fold_in(key_of[5], 71), 0),
        "widths": draw_widths(jax.random.fold_in(key_of[5], 71), 0),
        "w_query": draw_w_query(jax.random.fold_in(key_of[5], 71), 0),
        "w_keyval": draw_w_keyval(jax.random.fold_in(key_of[5], 71), 0),
        "w_out": scatter_about(key_of[4], (C, C), C ** -0.5, 0.25),
    }


MASKED_SCORE = -1e+30

def row_weight(row_ids, row_total):
    inside = (row_ids >= 0) & (row_ids < row_total)
    clipped = jnp.clip(row_ids, 0, row_total - 1).astype(jnp.float32)
    return jnp.where(inside, jnp.sin(jnp.pi * (clipped + 0.5) / row_total), jnp.zeros_like(clipped))

def log_weight(weight):
    return jnp.log(jnp.where(weight > 0, weight, jnp.ones_like(weight)))

def attend(queries, keyvals, allowed, key_logs):
    query_count = queries.shape[0]
    channels = queries.shape[1]
    query_heads = queries.astype(jnp.float32).reshape(query_count, HEADS, HDIM)
    key_heads = keyvals[:, :channels].astype(jnp.float32).reshape(-1, HEADS, HDIM)
    value_heads = keyvals[:, channels:].astype(jnp.float32).reshape(-1, HEADS, HDIM)
    score_scale = 1.0 / math.sqrt(HDIM)
    scores = jnp.einsum('qhd,khd->hqk', query_heads, key_heads) * score_scale + key_logs[None, None, :]
    scores = jnp.where(allowed[None], scores, MASKED_SCORE)
    row_max = lax.optimization_barrier(jnp.max(scores, axis=2, keepdims=True))
    exp_scores = jnp.exp(scores - row_max)
    denominator = lax.optimization_barrier(jnp.sum(exp_scores, axis=2))
    rounded = lax.optimization_barrier(exp_scores.astype(jnp.bfloat16)).astype(jnp.float32)
    weighted = jnp.einsum('hqk,khd->qhd', rounded, value_heads)
    result = weighted / jnp.transpose(denominator)[:, :, None]
    return result.reshape(query_count, channels).astype(jnp.bfloat16)

def reference(grid_features, widths, w_query, w_keyval, w_out):
    row_ids = jnp.arange(NLAT, dtype=jnp.int32)
    upper_weight = row_weight(row_ids - 1, NLAT)[:, None, None]
    lower_weight = row_weight(row_ids + 1, NLAT)[:, None, None]
    as_float = grid_features.astype(jnp.float32)
    upper_row = jnp.roll(as_float, 1, axis=0)
    lower_row = jnp.roll(as_float, -1, axis=0)
    lat_mix = ((upper_weight * upper_row + lower_weight * lower_row) / (upper_weight + lower_weight)).astype(jnp.bfloat16)
    west_col = jnp.roll(as_float, 1, axis=1)
    east_col = jnp.roll(as_float, -1, axis=1)
    lon_mix = (0.5 * (west_col + east_col)).astype(jnp.bfloat16)
    basis_cat = jnp.concatenate([grid_features, lat_mix, lon_mix], axis=2).reshape(-1, 3 * C)
    keyval = jnp.dot(basis_cat, w_keyval, preferred_element_type=jnp.float32).astype(jnp.bfloat16)
    keyval = keyval.reshape(NLAT, NLON, 2 * C)
    queries = jnp.dot(grid_features.reshape(-1, C), w_query, preferred_element_type=jnp.float32)
    queries = queries.astype(jnp.bfloat16).reshape(NLAT, NLON, C)
    padded = jnp.pad(keyval, ((1, 1), (0, 0), (0, 0)))
    wrapped = jnp.concatenate([padded[:, NLON - LON_DEV:], padded, padded[:, :LON_DEV]], axis=1)
    padded_ids = jnp.arange(-1, NLAT + 1, dtype=jnp.int32)
    padded_weight = row_weight(padded_ids, NLAT)
    padded_valid = padded_weight > 0
    padded_log = log_weight(padded_weight)
    poles = jnp.stack([keyval[0], keyval[NLAT - 1]])
    lon_offsets = jnp.arange(LON_DEV, dtype=jnp.int32)

    def one_block(row_index, block_index, source, first_col, key_count, first_global):
        zero = jnp.zeros((), jnp.int32)
        query_cols = block_index * LON_DEV + lon_offsets
        query_block = lax.dynamic_slice(queries, (row_index, block_index * LON_DEV, zero), (1, LON_DEV, C))[0]
        near_part = lax.dynamic_slice(source, (row_index, first_col, zero), (3, key_count, 2 * C))
        near_part = near_part.reshape(3 * key_count, 2 * C)
        row_valid = lax.dynamic_slice_in_dim(padded_valid, row_index, 3)
        row_logs = lax.dynamic_slice_in_dim(padded_log, row_index, 3)
        half_width = lax.dynamic_slice_in_dim(widths, row_index, 1)[0]
        key_cols = jnp.mod(first_global + jnp.arange(key_count, dtype=jnp.int32), NLON)
        forward_gap = jnp.mod(key_cols[None, :] - query_cols[:, None], NLON)
        distance = jnp.minimum(forward_gap, NLON - forward_gap)
        allowed = row_valid[None, :, None] & (distance[:, None, :] <= half_width)
        allowed = allowed.reshape(LON_DEV, 3 * key_count)
        key_logs = jnp.repeat(row_logs, key_count)
        pole_part = lax.dynamic_slice(poles, (zero, block_index * LON_DEV, zero), (2, LON_DEV, 2 * C))
        pole_part = pole_part.reshape(2 * LON_DEV, 2 * C)
        all_keys = jnp.concatenate([near_part, pole_part], axis=0)
        all_allowed = jnp.concatenate([allowed, jnp.ones((LON_DEV, 2 * LON_DEV), dtype=bool)], axis=1)
        all_logs = jnp.concatenate([key_logs, jnp.zeros((2 * LON_DEV,), key_logs.dtype)])
        return attend(query_block, all_keys, all_allowed, all_logs)

    def window(item_index):
        row_index = item_index // N_LON
        block_index = item_index % N_LON
        return one_block(row_index, block_index, wrapped, block_index * LON_DEV, 3 * LON_DEV, block_index * LON_DEV - LON_DEV)
    attended = lax.map(window, jnp.arange(NLAT * N_LON, dtype=jnp.int32)).reshape(NLAT, NLON, C)

    def full_row(item_index):
        row_index = jnp.where(item_index < N_LON, 0, NLAT - 1).astype(jnp.int32)
        block_index = item_index % N_LON
        return one_block(row_index, block_index, padded, jnp.zeros((), jnp.int32), NLON, jnp.zeros((), jnp.int32))
    polar = lax.map(full_row, jnp.arange(2 * N_LON, dtype=jnp.int32)).reshape(2, NLON, C)
    attended = attended.at[0].set(polar[0]).at[NLAT - 1].set(polar[1])
    layer_out = jnp.dot(attended.reshape(-1, C), w_out, preferred_element_type=jnp.float32)
    return layer_out.astype(jnp.bfloat16).reshape(NLAT, NLON, C)
```

```python
import jax
import jax.numpy as jnp
import numpy as np
from jax import lax
from jax.experimental import pallas as pl
from jax.experimental.pallas import tpu as pltpu
from jax.sharding import PartitionSpec as P

HEADS = 8
HDIM = 64
PAIRS = 4
LANES = 128
MASKED = -1e30
F32 = jnp.float32
BF16 = jnp.bfloat16
VMEM = pl.BlockSpec(memory_space=pltpu.VMEM)
SMEM = pl.BlockSpec(memory_space=pltpu.SMEM)
PARAMS = pltpu.CompilerParams(vmem_limit_bytes=48 * 1024 * 1024)


def cost(flops, nbytes):
    return pl.CostEstimate(flops=flops, bytes_accessed=nbytes, transcendentals=0)


def row_weight(row_ids, row_total):
    inside = (row_ids >= 0) & (row_ids < row_total)
    clipped = jnp.clip(row_ids, 0, row_total - 1).astype(F32)
    return jnp.where(inside, jnp.sin(jnp.pi * (clipped + 0.5) / row_total), jnp.zeros_like(clipped))


def lane_ids(shape):
    return lax.broadcasted_iota(jnp.int32, shape, len(shape) - 1)


def dot_nn(a, b):
    return lax.dot_general(a, b, (((1,), (0,)), ((), ())), preferred_element_type=F32)


def dot_nt(a, b):
    return lax.dot_general(a, b, (((1,), (1,)), ((), ())), preferred_element_type=F32)


def three_parts(x):
    a = x.astype(BF16)
    rest = x - a.astype(F32)
    b = rest.astype(BF16)
    c = (rest - b.astype(F32)).astype(BF16)
    return a.astype(F32), b.astype(F32), c.astype(F32)


def early_kernel(f_ref, wq_ref, wk_ref, q_ref, base_ref):
    f = f_ref[...].reshape(256, 512)
    q = dot_nn(f, wq_ref[...]).astype(BF16) * jnp.asarray(HDIM ** -0.5, BF16)
    for p in range(PAIRS):
        q_ref[p] = q[:, p * LANES : (p + 1) * LANES].reshape(2, 128, LANES)
    base_ref[...] = dot_nn(f, wk_ref[...])


def keyval_kernel(coef_ref, f_ref, up_ref, dn_ref, west_ref, east_ref, base_ref, w1_ref, w2_ref, kv_ref):
    rows = [up_ref[0], f_ref[0], f_ref[1], dn_ref[0]]
    rows = [r.astype(F32) for r in rows]
    cell = lax.broadcasted_iota(jnp.int32, (128, 512), 0)
    lat, lon = [], []
    for r in range(2):
        lat.append((coef_ref[2 * r] * rows[r] + coef_ref[2 * r + 1] * rows[r + 2]).astype(BF16))
        mid = rows[r + 1]
        w = jnp.where(cell == 0, west_ref[r].astype(F32), pltpu.roll(mid, 1, 0))
        e = jnp.where(cell == 127, east_ref[r].astype(F32), pltpu.roll(mid, 127, 0))
        lon.append((0.5 * (w + e)).astype(BF16))
    lat = jnp.concatenate(lat, axis=0)
    lon = jnp.concatenate(lon, axis=0)
    low = lane_ids((256, LANES)) < HDIM
    for p in range(PAIRS):
        parts = []
        for side in range(2):
            c = slice(512 * side + p * LANES, 512 * side + (p + 1) * LANES)
            parts.append(base_ref[:, c] + dot_nn(lat, w1_ref[:, c]) + dot_nn(lon, w2_ref[:, c]))
        k, v = parts
        v = pltpu.roll(v, HDIM, 1)
        kv_ref[2 * p] = jnp.where(low, k, v).astype(BF16).reshape(2, 128, LANES)
        kv_ref[2 * p + 1] = jnp.where(low, v, k).astype(BF16).reshape(2, 128, LANES)


def window_kernel(
    width_ref, log_ref, q_ref, qn_ref, qs_ref, kv_ref, kvw_ref, kve_ref, pn_ref, ps_ref,
    o_ref, st_ref, rn_ref, rs_ref, bias_a, bias_b,
):
    ahead = lax.broadcasted_iota(jnp.int32, (128, 384), 1) - 128
    here = lax.broadcasted_iota(jnp.int32, (128, 384), 0)
    gap = jnp.abs(ahead - here)
    for t in range(4):
        inside = gap <= width_ref[t]
        if t < 3:
            bias_a[t * 128 : (t + 1) * 128] = jnp.where(inside, log_ref[0], MASKED)
        if t > 0:
            bias_b[(t - 1) * 128 : t * 128] = jnp.where(inside, log_ref[1], MASKED)
    low = lane_ids((128, LANES)) < HDIM
    lane = lane_ids((128, LANES))
    ones = jnp.ones((384, LANES), BF16)
    stats = [jnp.zeros((128, LANES), F32) for _ in range(4)]
    for p in range(PAIRS):
        halves = []
        for odd in range(2):
            h = 2 * p + odd
            keep = (lane >= HDIM) if odd else low
            qs = [qn_ref[p], q_ref[p, 0], q_ref[p, 1], qs_ref[p]]
            qs = [jnp.where(keep, x, jnp.zeros_like(x)) for x in qs]
            kva = jnp.concatenate([kvw_ref[h, 0], kv_ref[h, 0], kve_ref[h, 0]], axis=0)
            kvb = jnp.concatenate([kvw_ref[h, 1], kv_ref[h, 1], kve_ref[h, 1]], axis=0)
            kvp = jnp.concatenate([pn_ref[h], ps_ref[h]], axis=0)
            sa = dot_nt(jnp.concatenate(qs[:3], axis=0), kva) + bias_a[...]
            sb = dot_nt(jnp.concatenate(qs[1:], axis=0), kvb) + bias_b[...]
            sp = dot_nt(jnp.concatenate(qs[1:3], axis=0), kvp)
            ma = jnp.max(sa, axis=1, keepdims=True)
            mb = jnp.max(sb, axis=1, keepdims=True)
            mp = jnp.max(sp, axis=1, keepdims=True)
            mid = jnp.maximum(jnp.maximum(ma[128:], mb[:256]), mp)
            mn = ma[:128]
            ms = mb[256:]
            pa = jnp.exp(sa - jnp.concatenate([mn, mid], axis=0)).astype(BF16)
            pb = jnp.exp(sb - jnp.concatenate([mid, ms], axis=0)).astype(BF16)
            pp = jnp.exp(sp - mid).astype(BF16)
            oa = dot_nn(pa, jnp.concatenate([kva, ones], axis=1))
            ob = dot_nn(pb, jnp.concatenate([kvb, ones], axis=1))
            op = dot_nn(pp, jnp.concatenate([kvp, ones[:256]], axis=1))
            om = oa[128:] + ob[:256] + op
            full = [oa[:128], om[:128], om[128:], ob[256:]]
            tops = [mn, mid[:128], mid[128:], ms]
            halves.append([x[:, :LANES] / x[:, LANES:] for x in full])
            for t in range(4):
                parts = three_parts(tops[t] + jnp.log(full[t][:, LANES:]))
                for i in range(3):
                    stats[t] = jnp.where(lane == 3 * h + i, parts[i], stats[t])
        both = [jnp.where(low, halves[1][t], halves[0][t]) for t in range(4)]
        rn_ref[p] = both[0].astype(BF16)
        o_ref[p, 0] = both[1]
        o_ref[p, 1] = both[2]
        rs_ref[p] = both[3].astype(BF16)
    rn_ref[PAIRS] = stats[0].astype(BF16)
    st_ref[0] = stats[1].astype(BF16)
    st_ref[1] = stats[2].astype(BF16)
    rs_ref[PAIRS] = stats[3].astype(BF16)


def polar_kernel(odd_ref, log_ref, q_ref, kv_ref, out_ref, wide):
    odd = odd_ref[0]
    wide[:, :LANES] = kv_ref[...].reshape(2048, LANES)
    wide[:, LANES:] = jnp.ones((2048, LANES), BF16)
    lane = lane_ids((128, LANES))
    keep = (lane // HDIM) == odd
    start = odd * HDIM

    def block(b, carry):
        q = q_ref[b]
        q = jnp.where(keep, q, jnp.zeros_like(q))
        s = dot_nt(q, wide[:, :LANES])
        m = jnp.max(s, axis=1, keepdims=True)
        e = jnp.exp(s - m).astype(BF16)
        full = dot_nn(e, wide[...])
        total = full[:, LANES:]
        out = full[:, :LANES] / total
        parts = three_parts(m + jnp.log(total) + log_ref[0])
        for i in range(3):
            out = jnp.where(lane == start + i, parts[i], out)
        out_ref[b] = out.astype(BF16)
        return carry

    lax.fori_loop(0, 8, block, 0, unroll=2)


def final_kernel(role_ref, o_ref, st_ref, ra_ref, rb_ref, p1_ref, p2_ref, wo_ref, out_ref, att):
    src = lax.broadcasted_iota(jnp.int32, (LANES, 512), 0) // 3
    dst = lax.broadcasted_iota(jnp.int32, (LANES, 512), 1)
    head = 2 * (dst // LANES) + jnp.where(dst % LANES < HDIM, 1, 0)
    pick = jnp.where(src == head, 1.0, 0.0).astype(BF16)
    for r, ret in ((0, ra_ref), (1, rb_ref)):
        lse = dot_nn(st_ref[r], pick)
        lse_ret = jnp.where(role_ref[r] == 1, MASKED, dot_nn(ret[PAIRS], pick))
        mine = jnp.concatenate([o_ref[p, r] for p in range(PAIRS)], axis=1)
        other = jnp.concatenate([ret[p] for p in range(PAIRS)], axis=1).astype(F32)
        other = jnp.where(role_ref[r] == 1, 0.0, other)
        top = jnp.maximum(lse, lse_ret)
        wa = jnp.exp(lse - top)
        wb = jnp.exp(lse_ret - top)
        att[r * 128 : (r + 1) * 128] = ((mine * wa + other * wb) / (wa + wb)).astype(BF16)

        @pl.when(role_ref[r] == 1)
        def _():
            lane = lane_ids((128, LANES))
            row = lax.broadcasted_iota(jnp.int32, (LANES, LANES), 0)
            col = lax.broadcasted_iota(jnp.int32, (LANES, LANES), 1)
            pick_even = jnp.where((row < 3) & (col >= HDIM), 1.0, 0.0).astype(BF16)
            pick_odd = jnp.where((row >= HDIM) & (row < HDIM + 3) & (col < HDIM), 1.0, 0.0).astype(BF16)
            for p in range(PAIRS):
                mo = o_ref[p, r]
                ml = lse[:, p * LANES : (p + 1) * LANES]
                vals, logs = [], []
                for ref in (p1_ref, p2_ref):
                    even, odd = ref[2 * p], ref[2 * p + 1]
                    vals.append(jnp.where(lane < HDIM, odd, even).astype(F32))
                    logs.append(dot_nn(even, pick_even) + dot_nn(odd, pick_odd))
                best = jnp.maximum(ml, jnp.maximum(logs[0], logs[1]))
                w0 = jnp.exp(ml - best)
                w1 = jnp.exp(logs[0] - best)
                w2 = jnp.exp(logs[1] - best)
                merged = (mo * w0 + vals[0] * w1 + vals[1] * w2) / (w0 + w1 + w2)
                att[r * 128 : (r + 1) * 128, p * LANES : (p + 1) * LANES] = merged.astype(BF16)

    order = []
    for p in range(PAIRS):
        order += [wo_ref[p * LANES + HDIM : (p + 1) * LANES], wo_ref[p * LANES : p * LANES + HDIM]]
    w = jnp.concatenate(order, axis=0)
    out_ref[...] = dot_nn(att[...], w).astype(BF16).reshape(2, 128, 512)


def call(kernel, outs, in_specs, flops, nbytes, scratch=()):
    return pl.pallas_call(
        kernel,
        out_shape=outs,
        grid=(1,),
        in_specs=in_specs,
        out_specs=jax.tree.map(lambda _: VMEM, outs),
        scratch_shapes=list(scratch),
        compiler_params=PARAMS,
        cost_estimate=cost(flops, nbytes),
    )


def sds(shape, dtype=BF16):
    return jax.ShapeDtypeStruct(shape, dtype)


def ring(n, k):
    return [(i, (i + k) % n) for i in range(n)]


def line(n, k):
    return [(i, i + k) for i in range(n) if 0 <= i + k < n]


def body(gf, widths, wq, wkv, wo):
    nlat, nlon = 16, 16
    total = 32
    li = lax.axis_index("lat")
    lj = lax.axis_index("lon")
    first = 2 * li
    even = li % 2 == 0
    swap = [(i, i ^ 1) for i in range(nlat)]
    groups = [list(range(8)), list(range(8, 16))]

    up = lax.ppermute(gf[1:2], "lat", line(nlat, 1))
    dn = lax.ppermute(gf[0:1], "lat", line(nlat, -1))
    west = lax.ppermute(gf[:, 127:], "lon", ring(nlon, 1))
    east = lax.ppermute(gf[:, :1], "lon", ring(nlon, -1))

    wspec = lambda b: pl.BlockSpec((512, 1024), lambda i: (b, 0))
    q, base = call(
        early_kernel,
        (sds((PAIRS, 2, 128, LANES)), sds((256, 1024), F32)),
        [VMEM, VMEM, wspec(0)],
        400_000_000, 3_000_000,
    )(gf, wq, wkv)

    rows = first + jnp.arange(2, dtype=jnp.int32)
    uw, lw = row_weight(rows - 1, total), row_weight(rows + 1, total)
    coef = jnp.stack([uw / (uw + lw), lw / (uw + lw)], axis=1).reshape(4)
    kv = call(
        keyval_kernel, sds((HEADS, 2, 128, LANES)),
        [SMEM] + [VMEM] * 6 + [wspec(1), wspec(2)],
        600_000_000, 4_000_000,
    )(coef, gf, up, dn, west, east, base, wkv, wkv)

    q_a, q_b = q[:, 0], q[:, 1]
    kv_a, kv_b = kv[:, 0], kv[:, 1]
    got_q = lax.ppermute(jnp.where(even, q_a, q_b), "lat", swap)
    got_kv = lax.ppermute(jnp.where(even, kv_b, kv_a), "lat", swap)
    polar_q = jnp.where(li == 0, q_a, jnp.where(li == nlat - 1, q_b, got_q))
    polar_kv = jnp.where(li == 0, kv_a, jnp.where(li == nlat - 1, kv_b, got_kv))
    all_kv = lax.all_to_all(jnp.concatenate([polar_kv, polar_kv], axis=0), "lon", 0, 0)
    all_q = lax.all_to_all(jnp.repeat(polar_q, 2, axis=0), "lon", 0, 0, axis_index_groups=groups)

    kvw = lax.ppermute(kv, "lon", ring(nlon, 1))
    kve = lax.ppermute(kv, "lon", ring(nlon, -1))
    qn = lax.ppermute(q_b, "lat", line(nlat, 1))
    qs = lax.ppermute(q_a, "lat", line(nlat, -1))

    x = jnp.where(li == nlat - 1, kv_b, kv_a)
    for pairs in (
        [(0, 8), (15, 7)],
        [(0, 4), (8, 12), (15, 11), (7, 3)],
        [(0, 2), (4, 6), (8, 10), (12, 14), (15, 13), (11, 9), (7, 5), (3, 1)],
    ):
        got = lax.ppermute(x, "lat", pairs)
        here = np.zeros(nlat, bool)
        here[[b for _, b in pairs]] = True
        x = jnp.where(jnp.asarray(here)[li], got, x)
    got = lax.ppermute(x, "lat", swap)
    pole_n = jnp.where(even, x, got)
    pole_s = jnp.where(even, got, x)

    near = first - 1 + jnp.arange(4, dtype=jnp.int32)
    reach = widths[jnp.clip(near, 0, total - 1)]
    reach = jnp.where((near <= 0) | (near >= total - 1), -1, reach)
    logs = jnp.log(row_weight(rows, total))
    o, st, ret_n, ret_s = call(
        window_kernel,
        (sds((PAIRS, 2, 128, LANES), F32), sds((2, 128, LANES)),
         sds((PAIRS + 1, 128, LANES)), sds((PAIRS + 1, 128, LANES))),
        [SMEM, SMEM] + [VMEM] * 8,
        8_000_000_000, 4_000_000,
        [pltpu.VMEM((384, 384), F32), pltpu.VMEM((384, 384), F32)],
    )(reach, logs, q, qn, qs, kv, kvw, kve, pole_n, pole_s)
    ret_b = lax.ppermute(ret_n, "lat", line(nlat, -1))
    ret_a = lax.ppermute(ret_s, "lat", line(nlat, 1))

    is_pole = (li == 0) | (li == nlat - 1)
    pole_log = jnp.log(row_weight(jnp.where(is_pole, 0, 1), total)).reshape(1)
    part = call(
        polar_kernel, sds((8, 128, LANES)), [SMEM, SMEM, VMEM, VMEM],
        6_000_000_000, 2_000_000, [pltpu.VMEM((2048, 2 * LANES), BF16)],
    )((lj % 2).reshape(1).astype(jnp.int32), pole_log, all_q, all_kv)
    part = lax.all_to_all(part, "lon", 0, 0, axis_index_groups=groups)
    part2 = lax.ppermute(part, "lat", swap)

    role = jnp.stack([li == 0, li == nlat - 1]).astype(jnp.int32)
    return call(
        final_kernel, sds((2, 128, 512)), [SMEM] + [VMEM] * 7,
        1_000_000_000, 3_000_000, [pltpu.VMEM((256, 512), BF16)],
    )(role, o, st, ret_a, ret_b, part, part2, wo)


def solution(mesh):
    in_specs = (P("lat", "lon", None), P(), P(), P(), P())
    return jax.shard_map(body, mesh=mesh, in_specs=in_specs, out_specs=P("lat", "lon", None), check_vma=False)
```

```python
import jax
import jax.numpy as jnp
import numpy as np
from jax import lax
from jax.experimental import pallas as pl
from jax.experimental.pallas import tpu as pltpu
from jax.sharding import PartitionSpec as P

HEADS = 8
HDIM = 64
NLAT = 32
PAIRS = 4
LANES = 128
MASKED = -1e30
F32 = jnp.float32
BF16 = jnp.bfloat16
VMEM = pl.BlockSpec(memory_space=pltpu.VMEM)
ANY = pl.BlockSpec(memory_space=pl.ANY)
SMEM = pl.BlockSpec(memory_space=pltpu.SMEM)
PARAMS = pltpu.CompilerParams(vmem_limit_bytes=20 * 1024 * 1024)


def cost(flops, nbytes):
    return pl.CostEstimate(flops=flops, bytes_accessed=nbytes, transcendentals=0)


def row_tables():
    weight = lambda row: np.sin(np.pi * (row + 0.5) / NLAT) if 0 <= row < NLAT else 0.0
    table = np.zeros((NLAT // 2, 8), np.float32)
    for band in range(NLAT // 2):
        step = 1 - 2 * (band % 2)
        w = [weight(2 * band + band % 2 + step * k) for k in (-1, 0, 1, 2)]
        table[band, :4] = w[0] / (w[0] + w[2]), w[2] / (w[0] + w[2]), w[1] / (w[1] + w[3]), w[3] / (w[1] + w[3])
        table[band, 4:6] = np.log(w[1]), np.log(w[2])
        table[band, 6] = np.log(weight(0 if band in (0, NLAT // 2 - 1) else 1))
    return table.reshape(-1)


def is_polar(band):
    return (band == 0) | (band == NLAT // 2 - 1)


def lane_ids(shape):
    return lax.broadcasted_iota(jnp.int32, shape, len(shape) - 1)


def dot_nn(a, b):
    return lax.dot_general(a, b, (((1,), (0,)), ((), ())), preferred_element_type=F32)


def dot_nt(a, b):
    return lax.dot_general(a, b, (((1,), (1,)), ((), ())), preferred_element_type=F32)


def dot_tn(a, b):
    return lax.dot_general(a, b, (((0,), (0,)), ((), ())), preferred_element_type=F32)


def half_turn(x):
    return pltpu.roll(x, HDIM, 1)


def three_parts(x):
    a = x.astype(BF16)
    rest = x - a.astype(F32)
    b = rest.astype(BF16)
    c = (rest - b.astype(F32)).astype(BF16)
    return a.astype(F32), b.astype(F32), c.astype(F32)


def edge_kernel(band_ref, f_ref, last_ref, lead_ref, sems):
    odd = band_ref[0] % 2
    copies = []
    for slot in range(2):
        row = f_ref.at[odd if slot == 0 else 1 - odd]
        copies.append(pltpu.make_async_copy(row.at[pl.ds(112, 16)], last_ref.at[slot], sems.at[2 * slot]))
        copies.append(pltpu.make_async_copy(row.at[pl.ds(0, 16)], lead_ref.at[slot], sems.at[2 * slot + 1]))
    for c in copies:
        c.start()
    for c in copies:
        c.wait()


def early_kernel(band_ref, f_ref, wq_ref, w_ref, qx_ref, qy_ref, pq_ref, base_ref):
    odd = band_ref[0] % 2
    low = lane_ids((64, LANES)) < HDIM
    f = jnp.concatenate([f_ref[odd], f_ref[1 - odd]], axis=0)
    q = dot_nn(f, wq_ref[...]).astype(BF16).astype(F32) * HDIM ** -0.5
    for p in range(PAIRS):
        block = q[:, p * LANES : (p + 1) * LANES]
        qx_ref[p] = block[:128].astype(BF16)
        qy_ref[p] = block[128:].astype(BF16)
        top, bottom = block[:64], block[64:128]
        pq_ref[2 * p] = jnp.where(low, top, half_turn(bottom)).astype(BF16)
        pq_ref[2 * p + 1] = jnp.where(low, half_turn(top), bottom).astype(BF16)
    base_ref[...] = dot_nn(f, w_ref[:512])


def keyval_kernel(
    band_ref, table_ref, f_ref, outer_ref, inner_ref, west_ref, east_ref, pq_ref, base_ref, w_ref,
    kv_ref, kvx_ref, mine_ref, swap_ref,
):
    band = band_ref[0]
    odd = band % 2
    coef = [table_ref[8 * band + i] for i in range(4)]
    own = [f_ref[odd], f_ref[1 - odd]]
    rows = [outer_ref[1 - odd].astype(F32), own[0].astype(F32), own[1].astype(F32), inner_ref[odd].astype(F32)]
    cell = lax.broadcasted_iota(jnp.int32, (128, 512), 0)
    lat, lon = [], []
    for r in range(2):
        lat.append((coef[2 * r] * rows[r] + coef[2 * r + 1] * rows[r + 2]).astype(BF16))
        mid = rows[r + 1]
        w = jnp.where(cell == 0, west_ref[r, 15:16].astype(F32), pltpu.roll(mid, 1, 0))
        e = jnp.where(cell == 127, east_ref[r, 0:1].astype(F32), pltpu.roll(mid, 127, 0))
        lon.append((0.5 * (w + e)).astype(BF16))
    basis = [jnp.concatenate(x, axis=0) for x in (lat, lon)]
    low = lane_ids((256, LANES)) < HDIM
    for p in range(PAIRS):
        parts = []
        for side in range(2):
            c = slice(512 * side + p * LANES, 512 * side + (p + 1) * LANES)
            parts.append(
                base_ref[:, c] + dot_nn(basis[0], w_ref[512:1024, c]) + dot_nn(basis[1], w_ref[1024:, c])
            )
        k, v = parts
        v = half_turn(v)
        for h, packed in ((2 * p, jnp.where(low, k, v)), (2 * p + 1, jnp.where(low, v, k))):
            packed = packed.astype(BF16)
            kv_ref[0, h] = packed[:128]
            kv_ref[1, h] = packed[128:]
            kvx_ref[h] = packed[:128]
            mine_ref[h, :128] = packed[:128]
            swap_ref[h, :128] = packed[128:]
    mine_ref[:, 128:] = pq_ref[...]
    swap_ref[:, 128:] = pq_ref[...]


def pick_kernel(band_ref, own_ref, got_ref, out_ref):
    picked = jnp.where(is_polar(band_ref[0]), own_ref[...], got_ref[...])
    out_ref[:HEADS] = picked
    out_ref[HEADS:] = picked


def window_kernel(
    band_ref, table_ref, width_ref, qo_ref, qx_ref, qy_ref, qi_ref, kv_ref, kvw_ref, kve_ref, p1_ref, p2_ref,
    o_ref, st_ref, ro_ref, ri_ref, bias_x, bias_y,
):
    ahead = lax.broadcasted_iota(jnp.int32, (128, 384), 1) - 128
    here = lax.broadcasted_iota(jnp.int32, (128, 384), 0)
    gap = jnp.abs(ahead - here)
    band = band_ref[0]
    first = 2 * band + band % 2
    step = 1 - 2 * (band % 2)
    for t in range(4):
        row = first + step * (t - 1)
        inner_row = (row > 0) & (row < NLAT - 1)
        inside = gap <= jnp.where(inner_row, width_ref[jnp.clip(row, 0, NLAT - 1)], -1)
        if t < 3:
            bias_x[t * 128 : (t + 1) * 128] = jnp.where(inside, table_ref[8 * band + 4], MASKED)
        if t > 0:
            bias_y[(t - 1) * 128 : t * 128] = jnp.where(inside, table_ref[8 * band + 5], MASKED)
    lane = lane_ids((128, LANES))
    low = lane < HDIM
    ones = jnp.ones((384, LANES), BF16)
    stats = [jnp.zeros((128, LANES), F32) for _ in range(4)]
    for p in range(PAIRS):
        halves = []
        for odd in range(2):
            h = 2 * p + odd
            keep = (lane >= HDIM) if odd else low
            qs = [qo_ref[p], qx_ref[p], qy_ref[p], qi_ref[p]]
            qs = [jnp.where(keep, x, jnp.zeros_like(x)) for x in qs]
            kva = jnp.concatenate([kvw_ref[0, h], kv_ref[0, h], kve_ref[0, h]], axis=0)
            kvb = jnp.concatenate([kvw_ref[1, h], kv_ref[1, h], kve_ref[1, h]], axis=0)
            kvp = jnp.concatenate([p1_ref[h], p2_ref[h]], axis=0)
            sa = dot_nt(jnp.concatenate(qs[:3], axis=0), kva) + bias_x[...]
            sb = dot_nt(jnp.concatenate(qs[1:], axis=0), kvb) + bias_y[...]
            sp = dot_nt(jnp.concatenate(qs[1:3], axis=0), kvp)
            ma = jnp.max(sa, axis=1, keepdims=True)
            mb = jnp.max(sb, axis=1, keepdims=True)
            mp = jnp.max(sp, axis=1, keepdims=True)
            mid = jnp.maximum(jnp.maximum(ma[128:], mb[:256]), mp)
            mo = ma[:128]
            mi = mb[256:]
            pa = jnp.exp(sa - jnp.concatenate([mo, mid], axis=0)).astype(BF16)
            pb = jnp.exp(sb - jnp.concatenate([mid, mi], axis=0)).astype(BF16)
            pp = jnp.exp(sp - mid).astype(BF16)
            oa = dot_nn(pa, jnp.concatenate([kva, ones], axis=1))
            ob = dot_nn(pb, jnp.concatenate([kvb, ones], axis=1))
            op = dot_nn(pp, jnp.concatenate([kvp, ones[:256]], axis=1))
            om = oa[128:] + ob[:256] + op
            full = [oa[:128], om[:128], om[128:], ob[256:]]
            tops = [mo, mid[:128], mid[128:], mi]
            halves.append([x[:, :LANES] / x[:, LANES:] for x in full])
            for t in range(4):
                parts = three_parts(tops[t] + jnp.log(full[t][:, LANES:]))
                for i in range(3):
                    stats[t] = jnp.where(lane == 3 * h + i, parts[i], stats[t])
        both = [jnp.where(low, halves[1][t], halves[0][t]) for t in range(4)]
        ro_ref[p] = both[0].astype(BF16)
        o_ref[p, 0] = both[1]
        o_ref[p, 1] = both[2]
        ri_ref[p] = both[3].astype(BF16)
    ro_ref[PAIRS] = stats[0].astype(BF16)
    st_ref[0] = stats[1].astype(BF16)
    st_ref[1] = stats[2].astype(BF16)
    ri_ref[PAIRS] = stats[3].astype(BF16)


def polar_kernel(band_ref, sector_ref, table_ref, in_ref, out_ref, wide, q_all, o_all, l_all):
    odd = sector_ref[0] % 2
    log = table_ref[8 * band_ref[0] + 6]
    lane = lane_ids((128, LANES))
    keep = (lane // HDIM) == odd
    low = lane_ids((64, LANES)) < HDIM
    first_sector = 8 * (sector_ref[0] // 8)
    for b in range(16):
        wide[128 * b : 128 * (b + 1), :LANES] = in_ref[b, :128]
    wide[:, LANES:] = jnp.ones((2048, LANES), BF16)
    for b in range(8):
        packed = in_ref[first_sector + b, 128:].astype(F32)
        turned = half_turn(packed)
        first = jnp.where(odd == 1, turned, packed)
        second = jnp.where(odd == 1, packed, turned)
        q = jnp.where(keep, jnp.concatenate([first, second], axis=0), 0.0)
        q_all[128 * b : 128 * (b + 1)] = q.astype(BF16)

    for b in range(4):
        rows = slice(256 * b, 256 * (b + 1))
        s = dot_nt(q_all[rows], wide[:, :LANES])
        m = jnp.max(s, axis=1, keepdims=True)
        e = jnp.exp(s - m).astype(BF16)
        full = dot_nn(e, wide[...])
        total = full[:, LANES:]
        o_all[rows] = full[:, :LANES] / total
        l_all[rows] = m + jnp.log(total) + log

    pick = jnp.where(
        lax.broadcasted_iota(jnp.int32, (16, LANES), 0) == lane_ids((16, LANES)), 1.0, 0.0
    ).astype(BF16)
    for b in range(8):
        out = o_all[128 * b : 128 * (b + 1)]
        turned = half_turn(out)
        left = jnp.where(odd == 1, out[:64], turned[:64])
        right = jnp.where(odd == 1, turned[64:], out[64:])
        out_ref[b, :64] = jnp.where(low, left, right).astype(BF16)
        parts = three_parts(l_all[128 * b : 128 * (b + 1)])
        stats = jnp.zeros((128, LANES), F32)
        for i in range(3):
            stats = jnp.where(lane == i, parts[i], stats)
        out_ref[b, 64:] = dot_nt(pick, stats.astype(BF16)).astype(BF16)


def final_kernel(band_ref, o_ref, st_ref, rx_ref, ry_ref, p1_ref, p2_ref, wo_ref, out_ref, att):
    odd = band_ref[0] % 2
    polar = is_polar(band_ref[0])
    src = lax.broadcasted_iota(jnp.int32, (LANES, 512), 0) // 3
    dst = lax.broadcasted_iota(jnp.int32, (LANES, 512), 1)
    head = 2 * (dst // LANES) + jnp.where(dst % LANES < HDIM, 1, 0)
    pick = jnp.where(src == head, 1.0, 0.0).astype(BF16)
    for r, ret in ((0, rx_ref), (1, ry_ref)):
        lse = dot_nn(st_ref[r], pick)
        lse_ret = dot_nn(ret[PAIRS], pick)
        mine = jnp.concatenate([o_ref[p, r] for p in range(PAIRS)], axis=1)
        other = jnp.concatenate([ret[p] for p in range(PAIRS)], axis=1).astype(F32)
        if r == 0:
            lse_ret = jnp.where(polar, MASKED, lse_ret)
            other = jnp.where(polar, 0.0, other)
        top = jnp.maximum(lse, lse_ret)
        wa = jnp.exp(lse - top)
        wb = jnp.exp(lse_ret - top)
        att[r * 128 : (r + 1) * 128] = ((mine * wa + other * wb) / (wa + wb)).astype(BF16)
        if r == 0:

            @pl.when(polar)
            def _():
                low = lane_ids((64, LANES)) < HDIM
                row = lax.broadcasted_iota(jnp.int32, (16, LANES), 0)
                col = lane_ids((16, LANES))
                pick_even = jnp.where((row < 3) & (col >= HDIM), 1.0, 0.0).astype(BF16)
                pick_odd = jnp.where((row < 3) & (col < HDIM), 1.0, 0.0).astype(BF16)
                for p in range(PAIRS):
                    ml = lse[:, p * LANES : (p + 1) * LANES]
                    vals, logs = [], []
                    for ref in (p1_ref, p2_ref):
                        even32, odd32 = ref[2 * p, :64].astype(F32), ref[2 * p + 1, :64].astype(F32)
                        first = jnp.where(low, odd32, half_turn(even32))
                        second = jnp.where(low, half_turn(odd32), even32)
                        vals.append(jnp.concatenate([first, second], axis=0))
                        logs.append(dot_tn(ref[2 * p, 64:], pick_even) + dot_tn(ref[2 * p + 1, 64:], pick_odd))
                    best = jnp.maximum(ml, jnp.maximum(logs[0], logs[1]))
                    w0 = jnp.exp(ml - best)
                    w1 = jnp.exp(logs[0] - best)
                    w2 = jnp.exp(logs[1] - best)
                    merged = (o_ref[p, 0] * w0 + vals[0] * w1 + vals[1] * w2) / (w0 + w1 + w2)
                    att[:128, p * LANES : (p + 1) * LANES] = merged.astype(BF16)

    order = []
    for p in range(PAIRS):
        order += [wo_ref[p * LANES + HDIM : (p + 1) * LANES], wo_ref[p * LANES : p * LANES + HDIM]]
    w = jnp.concatenate(order, axis=0)
    out = dot_nn(att[...], w).astype(BF16)
    out_ref[odd] = out[:128]
    out_ref[1 - odd] = out[128:]


def call(kernel, outs, in_specs, flops, nbytes, scratch=()):
    return pl.pallas_call(
        kernel,
        out_shape=outs,
        grid=(1,),
        in_specs=in_specs,
        out_specs=jax.tree.map(lambda _: VMEM, outs),
        scratch_shapes=list(scratch),
        compiler_params=PARAMS,
        cost_estimate=cost(flops, nbytes),
    )


def sds(shape, dtype=BF16):
    return jax.ShapeDtypeStruct(shape, dtype)


def ring(n, k):
    return [(i, (i + k) % n) for i in range(n)]


def body(gf, widths, wq, wkv, wo):
    nlat, nlon = NLAT // 2, 16
    li = lax.axis_index("lat").astype(jnp.int32)
    lj = lax.axis_index("lon").astype(jnp.int32)
    band, sector = li.reshape(1), lj.reshape(1)
    table = jnp.asarray(row_tables())
    inner = [(i, i ^ 1) for i in range(nlat)]
    outer = [(i, i + 1 if i % 2 else i - 1) for i in range(1, nlat - 1)]
    groups = [list(range(8)), list(range(8, 16))]

    last, lead = call(
        edge_kernel, (sds((2, 16, 512)), sds((2, 16, 512))), [SMEM, ANY], 1000, 100_000,
        [pltpu.SemaphoreType.DMA((4,))],
    )(band, gf)
    over = lax.ppermute(gf, "lat", outer)
    beside = lax.ppermute(gf, "lat", inner)
    west = lax.ppermute(last, "lon", ring(nlon, 1))
    east = lax.ppermute(lead, "lon", ring(nlon, -1))
    qx, qy, pq, base = call(
        early_kernel,
        (sds((PAIRS, 128, LANES)), sds((PAIRS, 128, LANES)), sds((HEADS, 64, LANES)), sds((256, 1024), F32)),
        [SMEM, VMEM, VMEM, VMEM],
        600_000_000, 6_000_000,
    )(band, gf, wq, wkv)

    kv, kvx, mine, swap = call(
        keyval_kernel,
        (sds((2, HEADS, 128, LANES)), sds((HEADS, 128, LANES)),
         sds((HEADS, 192, LANES)), sds((HEADS, 192, LANES))),
        [SMEM, SMEM] + [VMEM] * 8,
        1_000_000_000, 4_000_000,
    )(band, table, gf, over, beside, west, east, pq, base, wkv)

    got = lax.ppermute(swap, "lat", inner)
    picked = call(pick_kernel, sds((2 * HEADS, 192, LANES)), [SMEM, VMEM, VMEM], 1000, 1_000_000)(
        band, mine, got
    )
    all_polar = lax.all_to_all(picked, "lon", 0, 0)

    kv_later, all_polar = lax.optimization_barrier((kv, all_polar))
    kvw = lax.ppermute(kv_later, "lon", ring(nlon, 1))
    kve = lax.ppermute(kv_later, "lon", ring(nlon, -1))
    kvx, qx_later, qy_later, picked = lax.optimization_barrier((kvx, qx, qy, picked))
    qo = lax.ppermute(qx_later, "lat", outer)
    qi = lax.ppermute(qy_later, "lat", inner)

    even = li % 2 == 0
    x = kvx
    for pairs, here in (
        ([(0, 8), (15, 7)], jnp.where(even, li == 8, li == 7)),
        ([(0, 4), (8, 12), (15, 11), (7, 3)], li % 8 == jnp.where(even, 4, 3)),
        (
            [(0, 2), (4, 6), (8, 10), (12, 14), (15, 13), (11, 9), (7, 5), (3, 1)],
            li % 4 == jnp.where(even, 2, 1),
        ),
    ):
        x = jnp.where(here, lax.ppermute(x, "lat", pairs), x)
    x2 = lax.ppermute(x, "lat", inner)

    part = call(
        polar_kernel, sds((8, 80, LANES)), [SMEM, SMEM, SMEM, VMEM],
        6_000_000_000, 2_000_000,
        [pltpu.VMEM((2048, 2 * LANES), BF16), pltpu.VMEM((1024, LANES), BF16),
         pltpu.VMEM((1024, LANES), F32), pltpu.VMEM((1024, LANES), F32)],
    )(band, sector, table, all_polar)
    part = lax.all_to_all(part, "lon", 0, 0, axis_index_groups=groups)

    o, st, ret_o, ret_i = call(
        window_kernel,
        (sds((PAIRS, 2, 128, LANES), F32), sds((2, 128, LANES)),
         sds((PAIRS + 1, 128, LANES)), sds((PAIRS + 1, 128, LANES))),
        [SMEM, SMEM, SMEM] + [VMEM] * 9,
        8_000_000_000, 4_000_000,
        [pltpu.VMEM((384, 384), F32), pltpu.VMEM((384, 384), F32)],
    )(band, table, widths, qo, qx, qy, qi, kv, kvw, kve, x, x2)
    ret_x = lax.ppermute(ret_o, "lat", outer)
    ret_y = lax.ppermute(ret_i, "lat", inner)

    part, o = lax.optimization_barrier((part, o))
    part2 = lax.ppermute(part, "lat", inner)

    return call(
        final_kernel, sds((2, 128, 512)), [SMEM] + [VMEM] * 7,
        1_000_000_000, 3_000_000, [pltpu.VMEM((256, 512), BF16)],
    )(band, o, st, ret_x, ret_y, part, part2, wo)


def solution(mesh):
    in_specs = (P("lat", "lon", None), P(), P(), P(), P())
    return jax.shard_map(body, mesh=mesh, in_specs=in_specs, out_specs=P("lat", "lon", None), check_vma=False)
```

```python
import jax
import jax.numpy as jnp
import numpy as np
from jax import lax
from jax.experimental import pallas as pl
from jax.experimental.pallas import tpu as pltpu
from jax.sharding import PartitionSpec as P

HEADS = 8
HDIM = 64
NLAT = 32
PAIRS = 4
LANES = 128
MASKED = -1e30
F32 = jnp.float32
BF16 = jnp.bfloat16
VMEM = pl.BlockSpec(memory_space=pltpu.VMEM)
HBM = pl.BlockSpec(memory_space=pltpu.HBM)
SMEM = pl.BlockSpec(memory_space=pltpu.SMEM)
PARAMS = pltpu.CompilerParams(vmem_limit_bytes=20 * 1024 * 1024)


def cost(flops, nbytes):
    return pl.CostEstimate(flops=flops, bytes_accessed=nbytes, transcendentals=0)


def row_tables():
    weight = lambda row: np.sin(np.pi * (row + 0.5) / NLAT) if 0 <= row < NLAT else 0.0
    table = np.zeros((NLAT // 2, 8), np.float32)
    for band in range(NLAT // 2):
        step = 1 - 2 * (band % 2)
        w = [weight(2 * band + band % 2 + step * k) for k in (-1, 0, 1, 2)]
        table[band, :4] = w[0] / (w[0] + w[2]), w[2] / (w[0] + w[2]), w[1] / (w[1] + w[3]), w[3] / (w[1] + w[3])
        table[band, 4:6] = np.log(w[1]), np.log(w[2])
        table[band, 6] = np.log(weight(0 if band in (0, NLAT // 2 - 1) else 1))
    return table.reshape(-1)


def is_polar(band):
    return (band == 0) | (band == NLAT // 2 - 1)


def start_all(pairs, sems):
    copies = [pltpu.make_async_copy(src, dst, sems.at[i]) for i, (src, dst) in enumerate(pairs)]
    for c in copies:
        c.start()
    return copies


def wait_all(copies):
    for c in copies:
        c.wait()


def lane_ids(shape):
    return lax.broadcasted_iota(jnp.int32, shape, len(shape) - 1)


def dot_nn(a, b):
    return lax.dot_general(a, b, (((1,), (0,)), ((), ())), preferred_element_type=F32)


def dot_nt(a, b):
    return lax.dot_general(a, b, (((1,), (1,)), ((), ())), preferred_element_type=F32)


def dot_tn(a, b):
    return lax.dot_general(a, b, (((0,), (0,)), ((), ())), preferred_element_type=F32)


def half_turn(x):
    return pltpu.roll(x, HDIM, 1)


def three_parts(x):
    a = x.astype(BF16)
    rest = x - a.astype(F32)
    b = rest.astype(BF16)
    c = (rest - b.astype(F32)).astype(BF16)
    return a.astype(F32), b.astype(F32), c.astype(F32)


def edge_kernel(band_ref, f_ref, last_ref, lead_ref, sems):
    odd = band_ref[0] % 2
    pairs = []
    for slot, row in ((0, f_ref.at[odd]), (1, f_ref.at[1 - odd])):
        pairs += [(row.at[pl.ds(112, 16)], last_ref.at[slot]), (row.at[pl.ds(0, 16)], lead_ref.at[slot])]
    wait_all(start_all(pairs, sems))


def early_kernel(band_ref, f_ref, wq_ref, w_ref, qx_ref, qy_ref, pq_ref, base_ref):
    odd = band_ref[0] % 2
    low = lane_ids((64, LANES)) < HDIM
    f = jnp.concatenate([f_ref[odd], f_ref[1 - odd]], axis=0)
    q = dot_nn(f, wq_ref[...]).astype(BF16).astype(F32) * HDIM ** -0.5
    for p in range(PAIRS):
        block = q[:, p * LANES : (p + 1) * LANES]
        qx_ref[p] = block[:128].astype(BF16)
        qy_ref[p] = block[128:].astype(BF16)
        top, bottom = block[:64], block[64:128]
        pq_ref[2 * p] = jnp.where(low, top, half_turn(bottom)).astype(BF16)
        pq_ref[2 * p + 1] = jnp.where(low, half_turn(top), bottom).astype(BF16)
    base_ref[...] = dot_nn(f, w_ref[:512])


def keyval_kernel(
    band_ref, table_ref, f_ref, outer_ref, inner_ref, west_ref, east_ref, pq_ref, base_ref, w_ref,
    kv_ref, kvx_ref, mine_ref, swap_ref,
):
    band = band_ref[0]
    odd = band % 2
    coef = [table_ref[8 * band + i] for i in range(4)]
    for ref in (mine_ref, swap_ref):
        ref[:, 128:] = pq_ref[...]
    own = [f_ref[odd], f_ref[1 - odd]]
    rows = [outer_ref[1 - odd].astype(F32), own[0].astype(F32), own[1].astype(F32), inner_ref[odd].astype(F32)]
    cell = lax.broadcasted_iota(jnp.int32, (128, 512), 0)
    lat, lon = [], []
    for r in range(2):
        lat.append((coef[2 * r] * rows[r] + coef[2 * r + 1] * rows[r + 2]).astype(BF16))
        mid = rows[r + 1]
        before = jnp.where(cell == 0, west_ref[r, 15:16].astype(F32), pltpu.roll(mid, 1, 0))
        after = jnp.where(cell == 127, east_ref[r, 0:1].astype(F32), pltpu.roll(mid, 127, 0))
        lon.append((0.5 * (before + after)).astype(BF16))
    basis = [jnp.concatenate(x, axis=0) for x in (lat, lon)]
    low = lane_ids((256, LANES)) < HDIM
    for p in range(PAIRS):
        parts = []
        for side in range(2):
            c = slice(512 * side + p * LANES, 512 * side + (p + 1) * LANES)
            parts.append(
                base_ref[:, c] + dot_nn(basis[0], w_ref[512:1024, c]) + dot_nn(basis[1], w_ref[1024:, c])
            )
        k, v = parts
        v = half_turn(v)
        for h, packed in ((2 * p, jnp.where(low, k, v)), (2 * p + 1, jnp.where(low, v, k))):
            packed = packed.astype(BF16)
            kv_ref[0, h] = packed[:128]
            kv_ref[1, h] = packed[128:]
            kvx_ref[h] = packed[:128]
            mine_ref[h, :128] = packed[:128]
            swap_ref[h, :128] = packed[128:]


def pick_kernel(band_ref, own_ref, got_ref, out_ref):
    out_ref[...] = jnp.where(is_polar(band_ref[0]), own_ref[...], got_ref[...])


def window_kernel(
    band_ref, table_ref, width_ref, qo_ref, qx_ref, qy_ref, qi_ref, kv_ref, kvw_ref, kve_ref, p1_ref, p2_ref,
    o_ref, st_ref, ro_ref, ri_ref, bias_x, bias_y,
):
    ahead = lax.broadcasted_iota(jnp.int32, (128, 384), 1) - 128
    here = lax.broadcasted_iota(jnp.int32, (128, 384), 0)
    gap = jnp.abs(ahead - here)
    band = band_ref[0]
    first = 2 * band + band % 2
    step = 1 - 2 * (band % 2)
    for t in range(4):
        row = first + step * (t - 1)
        inner_row = (row > 0) & (row < NLAT - 1)
        inside = gap <= jnp.where(inner_row, width_ref[jnp.clip(row, 0, NLAT - 1)], -1)
        if t < 3:
            bias_x[t * 128 : (t + 1) * 128] = jnp.where(inside, table_ref[8 * band + 4], MASKED)
        if t > 0:
            bias_y[(t - 1) * 128 : t * 128] = jnp.where(inside, table_ref[8 * band + 5], MASKED)
    lane = lane_ids((128, LANES))
    low = lane < HDIM
    ones = jnp.ones((384, LANES), BF16)
    stats = [jnp.zeros((128, LANES), F32) for _ in range(4)]
    for p in range(PAIRS):
        halves = []
        for odd in range(2):
            h = 2 * p + odd
            keep = (lane >= HDIM) if odd else low
            qs = [qo_ref[p], qx_ref[p], qy_ref[p], qi_ref[p]]
            qs = [jnp.where(keep, x, jnp.zeros_like(x)) for x in qs]
            kva = jnp.concatenate([kvw_ref[0, h], kv_ref[0, h], kve_ref[0, h]], axis=0)
            kvb = jnp.concatenate([kvw_ref[1, h], kv_ref[1, h], kve_ref[1, h]], axis=0)
            kvp = jnp.concatenate([p1_ref[h], p2_ref[h]], axis=0)
            sa = dot_nt(jnp.concatenate(qs[:3], axis=0), kva) + bias_x[...]
            sb = dot_nt(jnp.concatenate(qs[1:], axis=0), kvb) + bias_y[...]
            sp = dot_nt(jnp.concatenate(qs[1:3], axis=0), kvp)
            ma = jnp.max(sa, axis=1, keepdims=True)
            mb = jnp.max(sb, axis=1, keepdims=True)
            mp = jnp.max(sp, axis=1, keepdims=True)
            mid = jnp.maximum(jnp.maximum(ma[128:], mb[:256]), mp)
            mo = ma[:128]
            mi = mb[256:]
            pa = jnp.exp(sa - jnp.concatenate([mo, mid], axis=0)).astype(BF16)
            pb = jnp.exp(sb - jnp.concatenate([mid, mi], axis=0)).astype(BF16)
            pp = jnp.exp(sp - mid).astype(BF16)
            oa = dot_nn(pa, jnp.concatenate([kva, ones], axis=1))
            ob = dot_nn(pb, jnp.concatenate([kvb, ones], axis=1))
            op = dot_nn(pp, jnp.concatenate([kvp, ones[:256]], axis=1))
            om = oa[128:] + ob[:256] + op
            full = [oa[:128], om[:128], om[128:], ob[256:]]
            tops = [mo, mid[:128], mid[128:], mi]
            halves.append([x[:, :LANES] / x[:, LANES:] for x in full])
            for t in range(4):
                parts = three_parts(tops[t] + jnp.log(full[t][:, LANES:]))
                for i in range(3):
                    stats[t] = jnp.where(lane == 3 * h + i, parts[i], stats[t])
        both = [jnp.where(low, halves[1][t], halves[0][t]) for t in range(4)]
        ro_ref[p] = both[0].astype(BF16)
        o_ref[p, 0] = both[1]
        o_ref[p, 1] = both[2]
        ri_ref[p] = both[3].astype(BF16)
    ro_ref[PAIRS] = stats[0].astype(BF16)
    st_ref[0] = stats[1].astype(BF16)
    st_ref[1] = stats[2].astype(BF16)
    ri_ref[PAIRS] = stats[3].astype(BF16)


def polar_near_kernel(band_ref, sector_ref, table_ref, in_ref, out_ref, wide, q_all, o_all, l_all):
    @pl.when((band_ref[0] < 2) | (band_ref[0] >= NLAT // 2 - 2))
    def _():
        queries = [in_ref[b, 128:] for b in range(8)]
        polar_part(band_ref, sector_ref, table_ref, in_ref, queries, out_ref, 0, wide, q_all, o_all, l_all)


def polar_far_kernel(band_ref, sector_ref, table_ref, in_ref, far_ref, part_ref, out_ref, wide, q_all, o_all, l_all):
    @pl.when((band_ref[0] < 2) | (band_ref[0] >= NLAT // 2 - 2))
    def _():
        near = 8 * (sector_ref[0] // 8)
        queries = [far_ref[b] for b in range(8)]
        polar_part(band_ref, sector_ref, table_ref, in_ref, queries, out_ref, 8 - near, wide, q_all, o_all, l_all)
        for b in range(8):
            out_ref[near + b] = part_ref[b]


def polar_part(band_ref, sector_ref, table_ref, in_ref, queries, out_ref, base, wide, q_all, o_all, l_all):
    odd = sector_ref[0] % 2
    log = table_ref[8 * band_ref[0] + 6]
    lane = lane_ids((128, LANES))
    keep = (lane // HDIM) == odd
    low = lane_ids((64, LANES)) < HDIM
    for b in range(8):
        wide[128 * b : 128 * (b + 1), :LANES] = in_ref[b, :128]
    wide[:, LANES:] = jnp.ones((1024, LANES), BF16)
    for b in range(8):
        packed = queries[b].astype(F32)
        turned = half_turn(packed)
        first = jnp.where(odd == 1, turned, packed)
        second = jnp.where(odd == 1, packed, turned)
        q = jnp.where(keep, jnp.concatenate([first, second], axis=0), 0.0)
        q_all[128 * b : 128 * (b + 1)] = q.astype(BF16)

    for b in range(4):
        rows = slice(256 * b, 256 * (b + 1))
        s = dot_nt(q_all[rows], wide[:, :LANES])
        m = jnp.max(s, axis=1, keepdims=True)
        e = jnp.exp(s - m).astype(BF16)
        full = dot_nn(e, wide[...])
        total = full[:, LANES:]
        o_all[rows] = full[:, :LANES] / total
        l_all[rows] = m + jnp.log(total) + log

    pick = jnp.where(
        lax.broadcasted_iota(jnp.int32, (16, LANES), 0) == lane_ids((16, LANES)), 1.0, 0.0
    ).astype(BF16)
    for b in range(8):
        out = o_all[128 * b : 128 * (b + 1)]
        turned = half_turn(out)
        left = jnp.where(odd == 1, out[:64], turned[:64])
        right = jnp.where(odd == 1, turned[64:], out[64:])
        out_ref[base + b, :64] = jnp.where(low, left, right).astype(BF16)
        parts = three_parts(l_all[128 * b : 128 * (b + 1)])
        stats = jnp.zeros((128, LANES), F32)
        for i in range(3):
            stats = jnp.where(lane == i, parts[i], stats)
        out_ref[base + b, 64:] = dot_nt(pick, stats.astype(BF16)).astype(BF16)


def final_kernel(band_ref, o_ref, st_ref, rx_ref, ry_ref, p1_ref, p2_ref, wo_ref, out_ref, att):
    odd = band_ref[0] % 2
    polar = is_polar(band_ref[0])
    src = lax.broadcasted_iota(jnp.int32, (LANES, 512), 0) // 3
    dst = lax.broadcasted_iota(jnp.int32, (LANES, 512), 1)
    head = 2 * (dst // LANES) + jnp.where(dst % LANES < HDIM, 1, 0)
    pick = jnp.where(src == head, 1.0, 0.0).astype(BF16)
    for r, ret in ((0, rx_ref), (1, ry_ref)):
        lse = dot_nn(st_ref[r], pick)
        lse_ret = dot_nn(ret[PAIRS], pick)
        mine = jnp.concatenate([o_ref[p, r] for p in range(PAIRS)], axis=1).astype(F32)
        other = jnp.concatenate([ret[p] for p in range(PAIRS)], axis=1).astype(F32)
        if r == 0:
            lse_ret = jnp.where(polar, MASKED, lse_ret)
            other = jnp.where(polar, 0.0, other)
        top = jnp.maximum(lse, lse_ret)
        wa = jnp.exp(lse - top)
        wb = jnp.exp(lse_ret - top)
        att[r * 128 : (r + 1) * 128] = ((mine * wa + other * wb) / (wa + wb)).astype(BF16)
        if r == 0:

            @pl.when(polar)
            def _():
                low = lane_ids((64, LANES)) < HDIM
                row = lax.broadcasted_iota(jnp.int32, (16, LANES), 0)
                col = lane_ids((16, LANES))
                pick_even = jnp.where((row < 3) & (col >= HDIM), 1.0, 0.0).astype(BF16)
                pick_odd = jnp.where((row < 3) & (col < HDIM), 1.0, 0.0).astype(BF16)
                for p in range(PAIRS):
                    ml = lse[:, p * LANES : (p + 1) * LANES]
                    vals, logs = [], []
                    for ref, h in ((p1_ref, 2 * p), (p1_ref, 8 + 2 * p), (p2_ref, 2 * p), (p2_ref, 8 + 2 * p)):
                        even32, odd32 = ref[h, :64].astype(F32), ref[h + 1, :64].astype(F32)
                        first = jnp.where(low, odd32, half_turn(even32))
                        second = jnp.where(low, half_turn(odd32), even32)
                        vals.append(jnp.concatenate([first, second], axis=0))
                        logs.append(dot_tn(ref[h, 64:], pick_even) + dot_tn(ref[h + 1, 64:], pick_odd))
                    vals.append(o_ref[p, 0].astype(F32))
                    logs.append(ml)
                    best = jnp.maximum(ml, jnp.maximum(jnp.maximum(logs[0], logs[1]), jnp.maximum(logs[2], logs[3])))
                    scales = [jnp.exp(x - best) for x in logs]
                    merged = sum(v * w for v, w in zip(vals, scales)) / sum(scales)
                    att[:128, p * LANES : (p + 1) * LANES] = merged.astype(BF16)

    order = []
    for p in range(PAIRS):
        order += [wo_ref[p * LANES + HDIM : (p + 1) * LANES], wo_ref[p * LANES : p * LANES + HDIM]]
    w = jnp.concatenate(order, axis=0)
    out = dot_nn(att[...], w).astype(BF16)
    out_ref[odd] = out[:128]
    out_ref[1 - odd] = out[128:]


def call(kernel, outs, in_specs, flops, nbytes, scratch=(), out_specs=None):
    return pl.pallas_call(
        kernel,
        out_shape=outs,
        grid=(1,),
        in_specs=in_specs,
        out_specs=out_specs or jax.tree.map(lambda _: VMEM, outs),
        scratch_shapes=list(scratch),
        compiler_params=PARAMS,
        cost_estimate=cost(flops, nbytes),
    )


def sds(shape, dtype=BF16):
    return jax.ShapeDtypeStruct(shape, dtype)


def ring(n, k):
    return [(i, (i + k) % n) for i in range(n)]


def body(gf, widths, wq, wkv, wo):
    nlat, nlon = NLAT // 2, 16
    li = lax.axis_index("lat").astype(jnp.int32)
    lj = lax.axis_index("lon").astype(jnp.int32)
    band, sector = li.reshape(1), lj.reshape(1)
    table = jnp.asarray(row_tables())
    inner = [(i, i ^ 1) for i in range(nlat)]
    outer = [(i, i + 1 if i % 2 else i - 1) for i in range(1, nlat - 1)]
    groups = [list(range(8)), list(range(8, 16))]

    last, lead = call(
        edge_kernel, (sds((2, 16, 512)), sds((2, 16, 512))), [SMEM, HBM], 8_000_000_000, 100_000,
        [pltpu.SemaphoreType.DMA((4,))],
    )(band, gf)
    over = lax.ppermute(gf, "lat", outer)
    beside = lax.ppermute(gf, "lat", inner)
    west = lax.ppermute(last, "lon", ring(nlon, 1))
    east = lax.ppermute(lead, "lon", ring(nlon, -1))
    qx, qy, pq, base = call(
        early_kernel,
        (sds((PAIRS, 128, LANES)), sds((PAIRS, 128, LANES)), sds((HEADS, 64, LANES)), sds((256, 1024), F32)),
        [SMEM, VMEM, VMEM, VMEM],
        600_000_000, 6_000_000,
    )(band, gf, wq, wkv)

    kv, kvx, mine, swap = call(
        keyval_kernel,
        (sds((2, HEADS, 128, LANES)), sds((HEADS, 128, LANES)),
         sds((HEADS, 192, LANES)), sds((HEADS, 192, LANES))),
        [SMEM, SMEM] + [VMEM] * 8,
        1_000_000_000, 4_000_000,
    )(band, table, gf, over, beside, west, east, pq, base, wkv)

    got = lax.ppermute(swap, "lat", inner)
    picked = call(pick_kernel, sds((HEADS, 192, LANES)), [SMEM] + [VMEM] * 2, 1000, 1_000_000)(
        band, mine, got
    )
    all_polar = lax.all_to_all(picked, "lon", 0, 0, axis_index_groups=groups)

    kvx, kv_later, picked = lax.optimization_barrier((kvx, kv, picked))
    kvw = lax.ppermute(kv_later, "lon", ring(nlon, 1))
    kve = lax.ppermute(kv_later, "lon", ring(nlon, -1))
    qo = lax.ppermute(qx, "lat", outer)
    qi = lax.ppermute(qy, "lat", inner)

    even = li % 2 == 0
    x = kvx
    for step in (4, 8, 12):
        got = lax.ppermute(kvx, "lat", [(0, step), (nlat - 1, nlat - 1 - step)])
        x = jnp.where(jnp.where(even, li, nlat - 1 - li) == step, got, x)
    got = lax.ppermute(x, "lat", [(i, i + 2) for i in range(0, 16, 4)] + [(i, i - 2) for i in range(3, 16, 4)])
    x = jnp.where(jnp.where(even, li, nlat - 1 - li) % 4 == 2, got, x)
    x, kvw, kve = lax.optimization_barrier((x, kvw, kve))
    x2 = lax.ppermute(x, "lat", inner)

    o, st, ret_o, ret_i = call(
        window_kernel,
        (sds((PAIRS, 2, 128, LANES), F32), sds((2, 128, LANES)),
         sds((PAIRS + 1, 128, LANES)), sds((PAIRS + 1, 128, LANES))),
        [SMEM, SMEM, SMEM] + [VMEM] * 9,
        1000, 1000,
        [pltpu.VMEM((384, 384), F32), pltpu.VMEM((384, 384), F32)],
    )(band, table, widths, qo, qx, qy, qi, kv, kvw, kve, x, x2)
    ret_x = lax.ppermute(ret_o, "lat", outer)
    ret_y = lax.ppermute(ret_i, "lat", inner)

    far = lax.ppermute(all_polar[:, 128:], "lon", [(i, i ^ 8) for i in range(nlon)])
    all_polar, st = lax.optimization_barrier((all_polar, st))
    scratch = [pltpu.VMEM((1024, 2 * LANES), BF16), pltpu.VMEM((1024, LANES), BF16),
               pltpu.VMEM((1024, LANES), F32), pltpu.VMEM((1024, LANES), F32)]
    part = call(
        polar_near_kernel, sds((8, 80, LANES)), [SMEM, SMEM, SMEM, VMEM], 5_000_000_000, 1_000_000, scratch
    )(band, sector, table, all_polar)
    part = call(
        polar_far_kernel, sds((16, 80, LANES)), [SMEM, SMEM, SMEM, VMEM, VMEM, VMEM],
        3_000_000_000, 1_000_000, scratch,
    )(band, sector, table, all_polar, far, part)
    part = lax.all_to_all(part, "lon", 0, 0)

    part, ret_x, ret_y = lax.optimization_barrier((part, ret_x, ret_y))
    part2 = lax.ppermute(part, "lat", inner)

    return call(
        final_kernel, sds((2, 128, 512)), [SMEM] + [VMEM] * 7,
        1_000_000_000, 3_000_000, [pltpu.VMEM((256, 512), BF16)],
    )(band, o, st, ret_x, ret_y, part, part2, wo)


def solution(mesh):
    in_specs = (P("lat", "lon", None), P(), P(), P(), P())
    return jax.shard_map(body, mesh=mesh, in_specs=in_specs, out_specs=P("lat", "lon", None), check_vma=False)
```

```python
import jax
import jax.numpy as jnp
import numpy as np
from jax import lax
from jax.experimental import pallas as pl
from jax.experimental.pallas import tpu as pltpu
from jax.sharding import PartitionSpec as P

HEADS = 8
HDIM = 64
NLAT = 32
PAIRS = 4
LANES = 128
MASKED = -1e30
F32 = jnp.float32
BF16 = jnp.bfloat16
VMEM = pl.BlockSpec(memory_space=pltpu.VMEM)
HBM = pl.BlockSpec(memory_space=pltpu.HBM)
SMEM = pl.BlockSpec(memory_space=pltpu.SMEM)
PARAMS = pltpu.CompilerParams(vmem_limit_bytes=20 * 1024 * 1024)


def cost(flops, nbytes):
    return pl.CostEstimate(flops=flops, bytes_accessed=nbytes, transcendentals=0)


def row_tables():
    weight = lambda row: np.sin(np.pi * (row + 0.5) / NLAT) if 0 <= row < NLAT else 0.0
    table = np.zeros((NLAT // 2, 8), np.float32)
    for band in range(NLAT // 2):
        step = 1 - 2 * (band % 2)
        w = [weight(2 * band + band % 2 + step * k) for k in (-1, 0, 1, 2)]
        table[band, :4] = w[0] / (w[0] + w[2]), w[2] / (w[0] + w[2]), w[1] / (w[1] + w[3]), w[3] / (w[1] + w[3])
        table[band, 4:6] = np.log(w[1]), np.log(w[2])
        table[band, 6] = np.log(weight(0 if band in (0, NLAT // 2 - 1) else 1))
    return table.reshape(-1)


def is_polar(band):
    return (band == 0) | (band == NLAT // 2 - 1)


def start_all(pairs, sems):
    copies = [pltpu.make_async_copy(src, dst, sems.at[i]) for i, (src, dst) in enumerate(pairs)]
    for c in copies:
        c.start()
    return copies


def wait_all(copies):
    for c in copies:
        c.wait()


def lane_ids(shape):
    return lax.broadcasted_iota(jnp.int32, shape, len(shape) - 1)


def dot_nn(a, b):
    return lax.dot_general(a, b, (((1,), (0,)), ((), ())), preferred_element_type=F32)


def dot_nt(a, b):
    return lax.dot_general(a, b, (((1,), (1,)), ((), ())), preferred_element_type=F32)


def dot_tn(a, b):
    return lax.dot_general(a, b, (((0,), (0,)), ((), ())), preferred_element_type=F32)


def half_turn(x):
    return pltpu.roll(x, HDIM, 1)


def three_parts(x):
    a = x.astype(BF16)
    rest = x - a.astype(F32)
    b = rest.astype(BF16)
    c = (rest - b.astype(F32)).astype(BF16)
    return a.astype(F32), b.astype(F32), c.astype(F32)


def edge_kernel(band_ref, f_ref, last_ref, lead_ref, sems):
    odd = band_ref[0] % 2
    pairs = []
    for slot, row in ((0, f_ref.at[odd]), (1, f_ref.at[1 - odd])):
        pairs += [(row.at[pl.ds(112, 16)], last_ref.at[slot]), (row.at[pl.ds(0, 16)], lead_ref.at[slot])]
    wait_all(start_all(pairs, sems))


def early_kernel(band_ref, f_ref, wq_ref, w_ref, qx_ref, qy_ref, pq_ref, base_ref):
    odd = band_ref[0] % 2
    low = lane_ids((64, LANES)) < HDIM
    f = jnp.concatenate([f_ref[odd], f_ref[1 - odd]], axis=0)
    q = dot_nn(f, wq_ref[...]).astype(BF16).astype(F32) * HDIM ** -0.5
    for p in range(PAIRS):
        block = q[:, p * LANES : (p + 1) * LANES]
        qx_ref[p] = block[:128].astype(BF16)
        qy_ref[p] = block[128:].astype(BF16)
        top, bottom = block[:64], block[64:128]
        pq_ref[2 * p] = jnp.where(low, top, half_turn(bottom)).astype(BF16)
        pq_ref[2 * p + 1] = jnp.where(low, half_turn(top), bottom).astype(BF16)
    base_ref[...] = dot_nn(f, w_ref[:512])


def keyval_kernel(
    band_ref, table_ref, f_ref, outer_ref, inner_ref, west_ref, east_ref, pq_ref, base_ref, w_ref,
    kv_ref, kvx_ref, mine_ref, swap_ref,
):
    band = band_ref[0]
    odd = band % 2
    coef = [table_ref[8 * band + i] for i in range(4)]
    for ref in (mine_ref, swap_ref):
        ref[:, 128:] = pq_ref[...]
    own = [f_ref[odd], f_ref[1 - odd]]
    rows = [outer_ref[1 - odd].astype(F32), own[0].astype(F32), own[1].astype(F32), inner_ref[odd].astype(F32)]
    cell = lax.broadcasted_iota(jnp.int32, (128, 512), 0)
    lat, lon = [], []
    for r in range(2):
        lat.append((coef[2 * r] * rows[r] + coef[2 * r + 1] * rows[r + 2]).astype(BF16))
        mid = rows[r + 1]
        before = jnp.where(cell == 0, west_ref[r, 15:16].astype(F32), pltpu.roll(mid, 1, 0))
        after = jnp.where(cell == 127, east_ref[r, 0:1].astype(F32), pltpu.roll(mid, 127, 0))
        lon.append((0.5 * (before + after)).astype(BF16))
    basis = [jnp.concatenate(x, axis=0) for x in (lat, lon)]
    low = lane_ids((256, LANES)) < HDIM
    for p in range(PAIRS):
        parts = []
        for side in range(2):
            c = slice(512 * side + p * LANES, 512 * side + (p + 1) * LANES)
            parts.append(
                base_ref[:, c] + dot_nn(basis[0], w_ref[512:1024, c]) + dot_nn(basis[1], w_ref[1024:, c])
            )
        k, v = parts
        v = half_turn(v)
        for h, packed in ((2 * p, jnp.where(low, k, v)), (2 * p + 1, jnp.where(low, v, k))):
            packed = packed.astype(BF16)
            kv_ref[0, h] = packed[:128]
            kv_ref[1, h] = packed[128:]
            kvx_ref[h] = packed[:128]
            mine_ref[h, :128] = packed[:128]
            swap_ref[h, :128] = packed[128:]


def pick_kernel(band_ref, own_ref, got_ref, out_ref):
    out_ref[...] = jnp.where(is_polar(band_ref[0]), own_ref[...], got_ref[...])


def window_kernel(
    band_ref, table_ref, width_ref, qo_ref, qx_ref, qy_ref, qi_ref, kv_ref, kvw_ref, kve_ref, p1_ref, p2_ref,
    o_ref, st_ref, ro_ref, ri_ref, bias_x, bias_y,
):
    ahead = lax.broadcasted_iota(jnp.int32, (128, 384), 1) - 128
    here = lax.broadcasted_iota(jnp.int32, (128, 384), 0)
    gap = jnp.abs(ahead - here)
    band = band_ref[0]
    first = 2 * band + band % 2
    step = 1 - 2 * (band % 2)
    for t in range(4):
        row = first + step * (t - 1)
        inner_row = (row > 0) & (row < NLAT - 1)
        inside = gap <= jnp.where(inner_row, width_ref[jnp.clip(row, 0, NLAT - 1)], -1)
        if t < 3:
            bias_x[t * 128 : (t + 1) * 128] = jnp.where(inside, table_ref[8 * band + 4], MASKED)
        if t > 0:
            bias_y[(t - 1) * 128 : t * 128] = jnp.where(inside, table_ref[8 * band + 5], MASKED)
    lane = lane_ids((128, LANES))
    low = lane < HDIM
    ones = jnp.ones((384, LANES), BF16)
    stats = [jnp.zeros((128, LANES), F32) for _ in range(4)]
    for p in range(PAIRS):
        halves = []
        for odd in range(2):
            h = 2 * p + odd
            keep = (lane >= HDIM) if odd else low
            qs = [qo_ref[p], qx_ref[p], qy_ref[p], qi_ref[p]]
            qs = [jnp.where(keep, x, jnp.zeros_like(x)) for x in qs]
            kva = jnp.concatenate([kvw_ref[0, h], kv_ref[0, h], kve_ref[0, h]], axis=0)
            kvb = jnp.concatenate([kvw_ref[1, h], kv_ref[1, h], kve_ref[1, h]], axis=0)
            kvp = jnp.concatenate([p1_ref[h], p2_ref[h]], axis=0)
            sa = dot_nt(jnp.concatenate(qs[:3], axis=0), kva) + bias_x[...]
            sb = dot_nt(jnp.concatenate(qs[1:], axis=0), kvb) + bias_y[...]
            sp = dot_nt(jnp.concatenate(qs[1:3], axis=0), kvp)
            ma = jnp.max(sa, axis=1, keepdims=True)
            mb = jnp.max(sb, axis=1, keepdims=True)
            mp = jnp.max(sp, axis=1, keepdims=True)
            mid = jnp.maximum(jnp.maximum(ma[128:], mb[:256]), mp)
            mo = ma[:128]
            mi = mb[256:]
            pa = jnp.exp(sa - jnp.concatenate([mo, mid], axis=0)).astype(BF16)
            pb = jnp.exp(sb - jnp.concatenate([mid, mi], axis=0)).astype(BF16)
            pp = jnp.exp(sp - mid).astype(BF16)
            oa = dot_nn(pa, jnp.concatenate([kva, ones], axis=1))
            ob = dot_nn(pb, jnp.concatenate([kvb, ones], axis=1))
            op = dot_nn(pp, jnp.concatenate([kvp, ones[:256]], axis=1))
            om = oa[128:] + ob[:256] + op
            full = [oa[:128], om[:128], om[128:], ob[256:]]
            tops = [mo, mid[:128], mid[128:], mi]
            halves.append([x[:, :LANES] / x[:, LANES:] for x in full])
            for t in range(4):
                parts = three_parts(tops[t] + jnp.log(full[t][:, LANES:]))
                for i in range(3):
                    stats[t] = jnp.where(lane == 3 * h + i, parts[i], stats[t])
        both = [jnp.where(low, halves[1][t], halves[0][t]) for t in range(4)]
        ro_ref[p] = both[0].astype(BF16)
        o_ref[p, 0] = both[1]
        o_ref[p, 1] = both[2]
        ri_ref[p] = both[3].astype(BF16)
    ro_ref[PAIRS] = stats[0].astype(BF16)
    st_ref[0] = stats[1].astype(BF16)
    st_ref[1] = stats[2].astype(BF16)
    ri_ref[PAIRS] = stats[3].astype(BF16)


def polar_near_kernel(band_ref, sector_ref, table_ref, in_ref, out_ref, wide, q_all, o_all, l_all):
    @pl.when((band_ref[0] < 2) | (band_ref[0] >= NLAT // 2 - 2))
    def _():
        queries = [in_ref[b, 128:] for b in range(8)]
        polar_part(band_ref, sector_ref, table_ref, in_ref, queries, out_ref, 0, wide, q_all, o_all, l_all)


def polar_far_kernel(band_ref, sector_ref, table_ref, in_ref, far_ref, part_ref, out_ref, wide, q_all, o_all, l_all):
    @pl.when((band_ref[0] < 2) | (band_ref[0] >= NLAT // 2 - 2))
    def _():
        near = 8 * (sector_ref[0] // 8)
        queries = [far_ref[b] for b in range(8)]
        polar_part(band_ref, sector_ref, table_ref, in_ref, queries, out_ref, 8 - near, wide, q_all, o_all, l_all)
        for b in range(8):
            out_ref[near + b] = part_ref[b]


def polar_part(band_ref, sector_ref, table_ref, in_ref, queries, out_ref, base, wide, q_all, o_all, l_all):
    odd = sector_ref[0] % 2
    log = table_ref[8 * band_ref[0] + 6]
    lane = lane_ids((128, LANES))
    keep = (lane // HDIM) == odd
    low = lane_ids((64, LANES)) < HDIM
    for b in range(8):
        wide[128 * b : 128 * (b + 1), :LANES] = in_ref[b, :128]
    wide[:, LANES:] = jnp.ones((1024, LANES), BF16)
    for b in range(8):
        packed = queries[b].astype(F32)
        turned = half_turn(packed)
        first = jnp.where(odd == 1, turned, packed)
        second = jnp.where(odd == 1, packed, turned)
        q = jnp.where(keep, jnp.concatenate([first, second], axis=0), 0.0)
        q_all[128 * b : 128 * (b + 1)] = q.astype(BF16)

    for b in range(4):
        rows = slice(256 * b, 256 * (b + 1))
        s = dot_nt(q_all[rows], wide[:, :LANES])
        m = jnp.max(s, axis=1, keepdims=True)
        e = jnp.exp(s - m).astype(BF16)
        full = dot_nn(e, wide[...])
        total = full[:, LANES:]
        o_all[rows] = full[:, :LANES] / total
        l_all[rows] = m + jnp.log(total) + log

    pick = jnp.where(
        lax.broadcasted_iota(jnp.int32, (16, LANES), 0) == lane_ids((16, LANES)), 1.0, 0.0
    ).astype(BF16)
    for b in range(8):
        out = o_all[128 * b : 128 * (b + 1)]
        turned = half_turn(out)
        left = jnp.where(odd == 1, out[:64], turned[:64])
        right = jnp.where(odd == 1, turned[64:], out[64:])
        out_ref[base + b, :64] = jnp.where(low, left, right).astype(BF16)
        parts = three_parts(l_all[128 * b : 128 * (b + 1)])
        stats = jnp.zeros((128, LANES), F32)
        for i in range(3):
            stats = jnp.where(lane == i, parts[i], stats)
        out_ref[base + b, 64:] = dot_nt(pick, stats.astype(BF16)).astype(BF16)


def final_kernel(band_ref, o_ref, st_ref, rx_ref, ry_ref, p1_ref, p2_ref, wo_ref, out_ref, att):
    odd = band_ref[0] % 2
    polar = is_polar(band_ref[0])
    src = lax.broadcasted_iota(jnp.int32, (LANES, 512), 0) // 3
    dst = lax.broadcasted_iota(jnp.int32, (LANES, 512), 1)
    head = 2 * (dst // LANES) + jnp.where(dst % LANES < HDIM, 1, 0)
    pick = jnp.where(src == head, 1.0, 0.0).astype(BF16)
    for r, ret in ((0, rx_ref), (1, ry_ref)):
        lse = dot_nn(st_ref[r], pick)
        lse_ret = dot_nn(ret[PAIRS], pick)
        mine = jnp.concatenate([o_ref[p, r] for p in range(PAIRS)], axis=1).astype(F32)
        other = jnp.concatenate([ret[p] for p in range(PAIRS)], axis=1).astype(F32)
        if r == 0:
            lse_ret = jnp.where(polar, MASKED, lse_ret)
            other = jnp.where(polar, 0.0, other)
        top = jnp.maximum(lse, lse_ret)
        wa = jnp.exp(lse - top)
        wb = jnp.exp(lse_ret - top)
        att[r * 128 : (r + 1) * 128] = ((mine * wa + other * wb) / (wa + wb)).astype(BF16)
        if r == 0:

            @pl.when(polar)
            def _():
                low = lane_ids((64, LANES)) < HDIM
                row = lax.broadcasted_iota(jnp.int32, (16, LANES), 0)
                col = lane_ids((16, LANES))
                pick_even = jnp.where((row < 3) & (col >= HDIM), 1.0, 0.0).astype(BF16)
                pick_odd = jnp.where((row < 3) & (col < HDIM), 1.0, 0.0).astype(BF16)
                for p in range(PAIRS):
                    ml = lse[:, p * LANES : (p + 1) * LANES]
                    vals, logs = [], []
                    for ref, h in ((p1_ref, 2 * p), (p1_ref, 8 + 2 * p), (p2_ref, 2 * p), (p2_ref, 8 + 2 * p)):
                        even32, odd32 = ref[h, :64].astype(F32), ref[h + 1, :64].astype(F32)
                        first = jnp.where(low, odd32, half_turn(even32))
                        second = jnp.where(low, half_turn(odd32), even32)
                        vals.append(jnp.concatenate([first, second], axis=0))
                        logs.append(dot_tn(ref[h, 64:], pick_even) + dot_tn(ref[h + 1, 64:], pick_odd))
                    vals.append(o_ref[p, 0].astype(F32))
                    logs.append(ml)
                    best = jnp.maximum(ml, jnp.maximum(jnp.maximum(logs[0], logs[1]), jnp.maximum(logs[2], logs[3])))
                    scales = [jnp.exp(x - best) for x in logs]
                    merged = sum(v * w for v, w in zip(vals, scales)) / sum(scales)
                    att[:128, p * LANES : (p + 1) * LANES] = merged.astype(BF16)

    order = []
    for p in range(PAIRS):
        order += [wo_ref[p * LANES + HDIM : (p + 1) * LANES], wo_ref[p * LANES : p * LANES + HDIM]]
    w = jnp.concatenate(order, axis=0)
    out = dot_nn(att[...], w).astype(BF16)
    out_ref[odd] = out[:128]
    out_ref[1 - odd] = out[128:]


def call(kernel, outs, in_specs, flops, nbytes, scratch=(), out_specs=None):
    return pl.pallas_call(
        kernel,
        out_shape=outs,
        grid=(1,),
        in_specs=in_specs,
        out_specs=out_specs or jax.tree.map(lambda _: VMEM, outs),
        scratch_shapes=list(scratch),
        compiler_params=PARAMS,
        cost_estimate=cost(flops, nbytes),
    )


def sds(shape, dtype=BF16):
    return jax.ShapeDtypeStruct(shape, dtype)


def ring(n, k):
    return [(i, (i + k) % n) for i in range(n)]


def body(gf, widths, wq, wkv, wo):
    nlat, nlon = NLAT // 2, 16
    li = lax.axis_index("lat").astype(jnp.int32)
    lj = lax.axis_index("lon").astype(jnp.int32)
    band, sector = li.reshape(1), lj.reshape(1)
    table = jnp.asarray(row_tables())
    inner = [(i, i ^ 1) for i in range(nlat)]
    outer = [(i, i + 1 if i % 2 else i - 1) for i in range(1, nlat - 1)]
    groups = [list(range(8)), list(range(8, 16))]

    last, lead = call(
        edge_kernel, (sds((2, 16, 512)), sds((2, 16, 512))), [SMEM, HBM], 8_000_000_000, 100_000,
        [pltpu.SemaphoreType.DMA((4,))],
    )(band, gf)
    over = lax.ppermute(gf, "lat", outer)
    beside = lax.ppermute(gf, "lat", inner)
    west = lax.ppermute(last, "lon", ring(nlon, 1))
    east = lax.ppermute(lead, "lon", ring(nlon, -1))
    qx, qy, pq, base = call(
        early_kernel,
        (sds((PAIRS, 128, LANES)), sds((PAIRS, 128, LANES)), sds((HEADS, 64, LANES)), sds((256, 1024), F32)),
        [SMEM, VMEM, VMEM, VMEM],
        600_000_000, 6_000_000,
    )(band, gf, wq, wkv)

    kv, kvx, mine, swap = call(
        keyval_kernel,
        (sds((2, HEADS, 128, LANES)), sds((HEADS, 128, LANES)),
         sds((HEADS, 192, LANES)), sds((HEADS, 192, LANES))),
        [SMEM, SMEM] + [VMEM] * 8,
        1_000_000_000, 4_000_000,
    )(band, table, gf, over, beside, west, east, pq, base, wkv)

    got = lax.ppermute(swap, "lat", inner)
    picked = call(pick_kernel, sds((HEADS, 192, LANES)), [SMEM] + [VMEM] * 2, 1000, 1_000_000)(
        band, mine, got
    )
    all_polar = lax.all_to_all(picked, "lon", 0, 0, axis_index_groups=groups)

    kvx, kv_later, picked = lax.optimization_barrier((kvx, kv, picked))
    kvw = lax.ppermute(kv_later, "lon", ring(nlon, 1))
    kve = lax.ppermute(kv_later, "lon", ring(nlon, -1))
    qo = lax.ppermute(qx, "lat", outer)
    qi = lax.ppermute(qy, "lat", inner)

    even = li % 2 == 0
    x = kvx
    for step in (4, 8, 12):
        got = lax.ppermute(kvx, "lat", [(0, step), (nlat - 1, nlat - 1 - step)])
        x = jnp.where(jnp.where(even, li, nlat - 1 - li) == step, got, x)
    got = lax.ppermute(x, "lat", [(i, i + 2) for i in range(0, 16, 4)] + [(i, i - 2) for i in range(3, 16, 4)])
    x = jnp.where(jnp.where(even, li, nlat - 1 - li) % 4 == 2, got, x)
    x, kvw, kve, qo, qi, all_polar = lax.optimization_barrier((x, kvw, kve, qo, qi, all_polar))
    x2 = lax.ppermute(x, "lat", inner)

    o, st, ret_o, ret_i = call(
        window_kernel,
        (sds((PAIRS, 2, 128, LANES), F32), sds((2, 128, LANES)),
         sds((PAIRS + 1, 128, LANES)), sds((PAIRS + 1, 128, LANES))),
        [SMEM, SMEM, SMEM] + [VMEM] * 9,
        1000, 1000,
        [pltpu.VMEM((384, 384), F32), pltpu.VMEM((384, 384), F32)],
    )(band, table, widths, qo, qx, qy, qi, kv, kvw, kve, x, x2)
    ret_x = lax.ppermute(ret_o, "lat", outer)
    ret_y = lax.ppermute(ret_i, "lat", inner)

    far = lax.ppermute(all_polar[:, 128:], "lon", [(i, i ^ 8) for i in range(nlon)])
    all_polar, st = lax.optimization_barrier((all_polar, st))
    scratch = [pltpu.VMEM((1024, 2 * LANES), BF16), pltpu.VMEM((1024, LANES), BF16),
               pltpu.VMEM((1024, LANES), F32), pltpu.VMEM((1024, LANES), F32)]
    part = call(
        polar_near_kernel, sds((8, 80, LANES)), [SMEM, SMEM, SMEM, VMEM], 5_000_000_000, 1_000_000, scratch
    )(band, sector, table, all_polar)
    part = call(
        polar_far_kernel, sds((16, 80, LANES)), [SMEM, SMEM, SMEM, VMEM, VMEM, VMEM],
        3_000_000_000, 1_000_000, scratch,
    )(band, sector, table, all_polar, far, part)
    part = lax.all_to_all(part, "lon", 0, 0)

    part, ret_x, ret_y = lax.optimization_barrier((part, ret_x, ret_y))
    part2 = lax.ppermute(part, "lat", inner)

    return call(
        final_kernel, sds((2, 128, 512)), [SMEM] + [VMEM] * 7,
        1_000_000_000, 3_000_000, [pltpu.VMEM((256, 512), BF16)],
    )(band, o, st, ret_x, ret_y, part, part2, wo)


def solution(mesh):
    in_specs = (P("lat", "lon", None), P(), P(), P(), P())
    return jax.shard_map(body, mesh=mesh, in_specs=in_specs, out_specs=P("lat", "lon", None), check_vma=False)
```

```python
import jax
import jax.numpy as jnp
import numpy as np
from jax import lax
from jax.experimental import pallas as pl
from jax.experimental.pallas import tpu as pltpu
from jax.sharding import PartitionSpec as P

HEADS = 8
HDIM = 64
NLAT = 32
PAIRS = 4
LANES = 128
MASKED = -1e30
F32 = jnp.float32
BF16 = jnp.bfloat16
VMEM = pl.BlockSpec(memory_space=pltpu.VMEM)
SMEM = pl.BlockSpec(memory_space=pltpu.SMEM)
PARAMS = pltpu.CompilerParams(vmem_limit_bytes=20 * 1024 * 1024)


def cost(flops, nbytes):
    return pl.CostEstimate(flops=flops, bytes_accessed=nbytes, transcendentals=0)


def row_tables():
    weight = lambda row: np.sin(np.pi * (row + 0.5) / NLAT) if 0 <= row < NLAT else 0.0
    table = np.zeros((NLAT // 2, 8), np.float32)
    for band in range(NLAT // 2):
        step = 1 - 2 * (band % 2)
        w = [weight(2 * band + band % 2 + step * k) for k in (-1, 0, 1, 2)]
        table[band, :4] = w[0] / (w[0] + w[2]), w[2] / (w[0] + w[2]), w[1] / (w[1] + w[3]), w[3] / (w[1] + w[3])
        table[band, 4:6] = np.log(w[1]), np.log(w[2])
        table[band, 6] = np.log(weight(0 if band in (0, NLAT // 2 - 1) else 1))
    return table.reshape(-1)


def is_polar(band):
    return (band == 0) | (band == NLAT // 2 - 1)


def lane_ids(shape):
    return lax.broadcasted_iota(jnp.int32, shape, len(shape) - 1)


def dot_nn(a, b):
    return lax.dot_general(a, b, (((1,), (0,)), ((), ())), preferred_element_type=F32)


def dot_nt(a, b):
    return lax.dot_general(a, b, (((1,), (1,)), ((), ())), preferred_element_type=F32)


def dot_tn(a, b):
    return lax.dot_general(a, b, (((0,), (0,)), ((), ())), preferred_element_type=F32)


def half_turn(x):
    return pltpu.roll(x, HDIM, 1)


def three_parts(x):
    a = x.astype(BF16)
    rest = x - a.astype(F32)
    b = rest.astype(BF16)
    c = (rest - b.astype(F32)).astype(BF16)
    return a.astype(F32), b.astype(F32), c.astype(F32)


def edge_kernel(band_ref, f_ref, fx_ref, fy_ref, last_ref, lead_ref):
    odd = band_ref[0] % 2
    for slot, out_ref in ((0, fx_ref), (1, fy_ref)):
        f = f_ref[odd if slot == 0 else 1 - odd]
        out_ref[...] = f
        last_ref[slot] = f[112:]
        lead_ref[slot] = f[:16]


def early_kernel(fx_ref, fy_ref, wq_ref, w_ref, qx_ref, qy_ref, pq_ref, base_ref):
    low = lane_ids((64, LANES)) < HDIM
    f = jnp.concatenate([fx_ref[...], fy_ref[...]], axis=0)
    q = dot_nn(f, wq_ref[...]).astype(BF16).astype(F32) * HDIM ** -0.5
    for p in range(PAIRS):
        block = q[:, p * LANES : (p + 1) * LANES]
        qx_ref[p] = block[:128].astype(BF16)
        qy_ref[p] = block[128:].astype(BF16)
        top, bottom = block[:64], block[64:128]
        pq_ref[2 * p] = jnp.where(low, top, half_turn(bottom)).astype(BF16)
        pq_ref[2 * p + 1] = jnp.where(low, half_turn(top), bottom).astype(BF16)
    base_ref[...] = dot_nn(f, w_ref[:512])


def keyval_kernel(
    band_ref, table_ref, fx_ref, fy_ref, outer_ref, inner_ref, west_ref, east_ref, pq_ref, base_ref, w_ref,
    kv_ref, kvx_ref, mine_ref, swap_ref,
):
    band = band_ref[0]
    coef = [table_ref[8 * band + i] for i in range(4)]
    for ref in (mine_ref, swap_ref):
        ref[:, 128:] = pq_ref[...]
    rows = [ref[...].astype(F32) for ref in (outer_ref, fx_ref, fy_ref, inner_ref)]
    cell = lax.broadcasted_iota(jnp.int32, (128, 512), 0)
    lat, lon = [], []
    for r in range(2):
        lat.append((coef[2 * r] * rows[r] + coef[2 * r + 1] * rows[r + 2]).astype(BF16))
        mid = rows[r + 1]
        before = jnp.where(cell == 0, west_ref[r, 15:16].astype(F32), pltpu.roll(mid, 1, 0))
        after = jnp.where(cell == 127, east_ref[r, 0:1].astype(F32), pltpu.roll(mid, 127, 0))
        lon.append((0.5 * (before + after)).astype(BF16))
    basis = [jnp.concatenate(x, axis=0) for x in (lat, lon)]
    low = lane_ids((256, LANES)) < HDIM
    for p in range(PAIRS):
        parts = []
        for side in range(2):
            c = slice(512 * side + p * LANES, 512 * side + (p + 1) * LANES)
            parts.append(
                base_ref[:, c] + dot_nn(basis[0], w_ref[512:1024, c]) + dot_nn(basis[1], w_ref[1024:, c])
            )
        k, v = parts
        v = half_turn(v)
        for h, packed in ((2 * p, jnp.where(low, k, v)), (2 * p + 1, jnp.where(low, v, k))):
            packed = packed.astype(BF16)
            kv_ref[0, h] = packed[:128]
            kv_ref[1, h] = packed[128:]
            kvx_ref[h] = packed[:128]
            mine_ref[h, :128] = packed[:128]
            swap_ref[h, :128] = packed[128:]


def pick_kernel(band_ref, own_ref, got_ref, out_ref):
    out_ref[...] = jnp.where(is_polar(band_ref[0]), own_ref[...], got_ref[...])


def window_kernel(
    band_ref, table_ref, width_ref, qo_ref, qx_ref, qy_ref, qi_ref, kv_ref, kvw_ref, kve_ref, p1_ref, p2_ref,
    o_ref, st_ref, ro_ref, ri_ref, bias_x, bias_y,
):
    ahead = lax.broadcasted_iota(jnp.int32, (128, 384), 1) - 128
    here = lax.broadcasted_iota(jnp.int32, (128, 384), 0)
    gap = jnp.abs(ahead - here)
    band = band_ref[0]
    first = 2 * band + band % 2
    step = 1 - 2 * (band % 2)
    for t in range(4):
        row = first + step * (t - 1)
        inner_row = (row > 0) & (row < NLAT - 1)
        inside = gap <= jnp.where(inner_row, width_ref[jnp.clip(row, 0, NLAT - 1)], -1)
        if t < 3:
            bias_x[t * 128 : (t + 1) * 128] = jnp.where(inside, table_ref[8 * band + 4], MASKED)
        if t > 0:
            bias_y[(t - 1) * 128 : t * 128] = jnp.where(inside, table_ref[8 * band + 5], MASKED)
    lane = lane_ids((128, LANES))
    low = lane < HDIM
    ones = jnp.ones((384, LANES), BF16)
    stats = [jnp.zeros((128, LANES), F32) for _ in range(4)]
    for p in range(PAIRS):
        halves = []
        for odd in range(2):
            h = 2 * p + odd
            keep = (lane >= HDIM) if odd else low
            qs = [qo_ref[p], qx_ref[p], qy_ref[p], qi_ref[p]]
            qs = [jnp.where(keep, x, jnp.zeros_like(x)) for x in qs]
            kva = jnp.concatenate([kvw_ref[0, h], kv_ref[0, h], kve_ref[0, h]], axis=0)
            kvb = jnp.concatenate([kvw_ref[1, h], kv_ref[1, h], kve_ref[1, h]], axis=0)
            kvp = jnp.concatenate([p1_ref[h], p2_ref[h]], axis=0)
            sa = dot_nt(jnp.concatenate(qs[:3], axis=0), kva) + bias_x[...]
            sb = dot_nt(jnp.concatenate(qs[1:], axis=0), kvb) + bias_y[...]
            sp = dot_nt(jnp.concatenate(qs[1:3], axis=0), kvp)
            ma = jnp.max(sa, axis=1, keepdims=True)
            mb = jnp.max(sb, axis=1, keepdims=True)
            mp = jnp.max(sp, axis=1, keepdims=True)
            mid = jnp.maximum(jnp.maximum(ma[128:], mb[:256]), mp)
            mo = ma[:128]
            mi = mb[256:]
            pa = jnp.exp(sa - jnp.concatenate([mo, mid], axis=0)).astype(BF16)
            pb = jnp.exp(sb - jnp.concatenate([mid, mi], axis=0)).astype(BF16)
            pp = jnp.exp(sp - mid).astype(BF16)
            oa = dot_nn(pa, jnp.concatenate([kva, ones], axis=1))
            ob = dot_nn(pb, jnp.concatenate([kvb, ones], axis=1))
            op = dot_nn(pp, jnp.concatenate([kvp, ones[:256]], axis=1))
            om = oa[128:] + ob[:256] + op
            full = [oa[:128], om[:128], om[128:], ob[256:]]
            tops = [mo, mid[:128], mid[128:], mi]
            halves.append([x[:, :LANES] / x[:, LANES:] for x in full])
            for t in range(4):
                parts = three_parts(tops[t] + jnp.log(full[t][:, LANES:]))
                for i in range(3):
                    stats[t] = jnp.where(lane == 3 * h + i, parts[i], stats[t])
        both = [jnp.where(low, halves[1][t], halves[0][t]) for t in range(4)]
        ro_ref[p] = both[0].astype(BF16)
        o_ref[p, 0] = both[1]
        o_ref[p, 1] = both[2]
        ri_ref[p] = both[3].astype(BF16)
    ro_ref[PAIRS] = stats[0].astype(BF16)
    st_ref[0] = stats[1].astype(BF16)
    st_ref[1] = stats[2].astype(BF16)
    ri_ref[PAIRS] = stats[3].astype(BF16)


def polar_near_kernel(band_ref, sector_ref, table_ref, in_ref, out_ref, wide, q_all, o_all, l_all):
    @pl.when((band_ref[0] < 2) | (band_ref[0] >= NLAT // 2 - 2))
    def _():
        queries = [in_ref[b, 128:] for b in range(8)]
        polar_part(band_ref, sector_ref, table_ref, in_ref, queries, out_ref, 0, wide, q_all, o_all, l_all)


def polar_far_kernel(band_ref, sector_ref, table_ref, in_ref, far_ref, part_ref, out_ref, wide, q_all, o_all, l_all):
    @pl.when((band_ref[0] < 2) | (band_ref[0] >= NLAT // 2 - 2))
    def _():
        near = 8 * (sector_ref[0] // 8)
        queries = [far_ref[b] for b in range(8)]
        polar_part(band_ref, sector_ref, table_ref, in_ref, queries, out_ref, 8 - near, wide, q_all, o_all, l_all)
        for b in range(8):
            out_ref[near + b] = part_ref[b]


def polar_part(band_ref, sector_ref, table_ref, in_ref, queries, out_ref, base, wide, q_all, o_all, l_all):
    odd = sector_ref[0] % 2
    log = table_ref[8 * band_ref[0] + 6]
    lane = lane_ids((128, LANES))
    keep = (lane // HDIM) == odd
    low = lane_ids((64, LANES)) < HDIM
    for b in range(8):
        wide[128 * b : 128 * (b + 1), :LANES] = in_ref[b, :128]
    wide[:, LANES:] = jnp.ones((1024, LANES), BF16)
    for b in range(8):
        packed = queries[b].astype(F32)
        turned = half_turn(packed)
        first = jnp.where(odd == 1, turned, packed)
        second = jnp.where(odd == 1, packed, turned)
        q = jnp.where(keep, jnp.concatenate([first, second], axis=0), 0.0)
        q_all[128 * b : 128 * (b + 1)] = q.astype(BF16)

    for b in range(4):
        rows = slice(256 * b, 256 * (b + 1))
        s = dot_nt(q_all[rows], wide[:, :LANES])
        m = jnp.max(s, axis=1, keepdims=True)
        e = jnp.exp(s - m).astype(BF16)
        full = dot_nn(e, wide[...])
        total = full[:, LANES:]
        o_all[rows] = full[:, :LANES] / total
        l_all[rows] = m + jnp.log(total) + log

    pick = jnp.where(
        lax.broadcasted_iota(jnp.int32, (16, LANES), 0) == lane_ids((16, LANES)), 1.0, 0.0
    ).astype(BF16)
    for b in range(8):
        out = o_all[128 * b : 128 * (b + 1)]
        turned = half_turn(out)
        left = jnp.where(odd == 1, out[:64], turned[:64])
        right = jnp.where(odd == 1, turned[64:], out[64:])
        out_ref[base + b, :64] = jnp.where(low, left, right).astype(BF16)
        parts = three_parts(l_all[128 * b : 128 * (b + 1)])
        stats = jnp.zeros((128, LANES), F32)
        for i in range(3):
            stats = jnp.where(lane == i, parts[i], stats)
        out_ref[base + b, 64:] = dot_nt(pick, stats.astype(BF16)).astype(BF16)


def head_pick():
    src = lax.broadcasted_iota(jnp.int32, (LANES, 512), 0) // 3
    dst = lax.broadcasted_iota(jnp.int32, (LANES, 512), 1)
    head = 2 * (dst // LANES) + jnp.where(dst % LANES < HDIM, 1, 0)
    return jnp.where(src == head, 1.0, 0.0).astype(BF16)


def turned_weights(wo_ref):
    order = []
    for p in range(PAIRS):
        order += [wo_ref[p * LANES + HDIM : (p + 1) * LANES], wo_ref[p * LANES : p * LANES + HDIM]]
    return jnp.concatenate(order, axis=0)


def merge_kernel(band_ref, o_ref, st_ref, rx_ref, ry_ref, wo_ref, out_ref, att):
    odd = band_ref[0] % 2
    pick = head_pick()
    for r, ret in ((0, rx_ref), (1, ry_ref)):
        lse = dot_nn(st_ref[r], pick)
        lse_ret = dot_nn(ret[PAIRS], pick)
        mine = jnp.concatenate([o_ref[p, r] for p in range(PAIRS)], axis=1)
        other = jnp.concatenate([ret[p] for p in range(PAIRS)], axis=1).astype(F32)
        top = jnp.maximum(lse, lse_ret)
        wa = jnp.exp(lse - top)
        wb = jnp.exp(lse_ret - top)
        att[r * 128 : (r + 1) * 128] = ((mine * wa + other * wb) / (wa + wb)).astype(BF16)
    out = dot_nn(att[...], turned_weights(wo_ref)).astype(BF16)
    out_ref[odd] = out[:128]
    out_ref[1 - odd] = out[128:]


def polar_row_kernel(band_ref, o_ref, st_ref, p1_ref, p2_ref, wo_ref, old_ref, out_ref, att, row_ref, sem):
    odd = band_ref[0] % 2

    @pl.when(is_polar(band_ref[0]))
    def _():
        lse = dot_nn(st_ref[0], head_pick())
        low = lane_ids((64, LANES)) < HDIM
        row = lax.broadcasted_iota(jnp.int32, (16, LANES), 0)
        col = lane_ids((16, LANES))
        pick_even = jnp.where((row < 3) & (col >= HDIM), 1.0, 0.0).astype(BF16)
        pick_odd = jnp.where((row < 3) & (col < HDIM), 1.0, 0.0).astype(BF16)
        for p in range(PAIRS):
            vals, logs = [o_ref[p, 0]], [lse[:, p * LANES : (p + 1) * LANES]]
            for ref, h in ((p1_ref, 2 * p), (p1_ref, 8 + 2 * p), (p2_ref, 2 * p), (p2_ref, 8 + 2 * p)):
                even32, odd32 = ref[h, :64].astype(F32), ref[h + 1, :64].astype(F32)
                first = jnp.where(low, odd32, half_turn(even32))
                second = jnp.where(low, half_turn(odd32), even32)
                vals.append(jnp.concatenate([first, second], axis=0))
                logs.append(dot_tn(ref[h, 64:], pick_even) + dot_tn(ref[h + 1, 64:], pick_odd))
            best = logs[0]
            for x in logs[1:]:
                best = jnp.maximum(best, x)
            scales = [jnp.exp(x - best) for x in logs]
            merged = sum(v * w for v, w in zip(vals, scales)) / sum(scales)
            att[:, p * LANES : (p + 1) * LANES] = merged.astype(BF16)
        row_ref[...] = dot_nn(att[...], turned_weights(wo_ref)).astype(BF16)
        copy = pltpu.make_async_copy(row_ref, out_ref.at[odd], sem)
        copy.start()
        copy.wait()


def call(kernel, outs, in_specs, flops, nbytes, scratch=(), out_specs=None):
    return pl.pallas_call(
        kernel,
        out_shape=outs,
        grid=(1,),
        in_specs=in_specs,
        out_specs=out_specs or jax.tree.map(lambda _: VMEM, outs),
        scratch_shapes=list(scratch),
        compiler_params=PARAMS,
        cost_estimate=cost(flops, nbytes),
    )


def sds(shape, dtype=BF16):
    return jax.ShapeDtypeStruct(shape, dtype)


def ring(n, k):
    return [(i, (i + k) % n) for i in range(n)]


def body(gf, widths, wq, wkv, wo):
    nlat, nlon = NLAT // 2, 16
    li = lax.axis_index("lat").astype(jnp.int32)
    lj = lax.axis_index("lon").astype(jnp.int32)
    band, sector = li.reshape(1), lj.reshape(1)
    table = jnp.asarray(row_tables())
    inner = [(i, i ^ 1) for i in range(nlat)]
    outer = [(i, i + 1 if i % 2 else i - 1) for i in range(1, nlat - 1)]
    groups = [list(range(8)), list(range(8, 16))]

    fx, fy, last, lead = call(
        edge_kernel,
        (sds((128, 512)), sds((128, 512)), sds((2, 16, 512)), sds((2, 16, 512))),
        [SMEM, VMEM], 8_000_000_000, 100_000,
    )(band, gf)
    over = lax.ppermute(fx, "lat", outer)
    beside = lax.ppermute(fy, "lat", inner)
    west = lax.ppermute(last, "lon", ring(nlon, 1))
    east = lax.ppermute(lead, "lon", ring(nlon, -1))
    qx, qy, pq, base = call(
        early_kernel,
        (sds((PAIRS, 128, LANES)), sds((PAIRS, 128, LANES)), sds((HEADS, 64, LANES)), sds((256, 1024), F32)),
        [VMEM] * 4,
        600_000_000, 6_000_000,
    )(fx, fy, wq, wkv)

    kv, kvx, mine, swap = call(
        keyval_kernel,
        (sds((2, HEADS, 128, LANES)), sds((HEADS, 128, LANES)),
         sds((HEADS, 192, LANES)), sds((HEADS, 192, LANES))),
        [SMEM, SMEM] + [VMEM] * 9,
        1_000_000_000, 4_000_000,
    )(band, table, fx, fy, over, beside, west, east, pq, base, wkv)

    got = lax.ppermute(swap, "lat", inner)
    picked = call(pick_kernel, sds((HEADS, 192, LANES)), [SMEM] + [VMEM] * 2, 1000, 1_000_000)(
        band, mine, got
    )
    all_polar = lax.all_to_all(picked, "lon", 0, 0, axis_index_groups=groups)

    kvx, kv_later, picked = lax.optimization_barrier((kvx, kv, picked))
    kvw = lax.ppermute(kv_later, "lon", ring(nlon, 1))
    kve = lax.ppermute(kv_later, "lon", ring(nlon, -1))
    qo = lax.ppermute(qx, "lat", outer)
    qi = lax.ppermute(qy, "lat", inner)

    even = li % 2 == 0
    x = kvx
    for step in (4, 8, 12):
        got = lax.ppermute(kvx, "lat", [(0, step), (nlat - 1, nlat - 1 - step)])
        x = jnp.where(jnp.where(even, li, nlat - 1 - li) == step, got, x)
    got = lax.ppermute(x, "lat", [(i, i + 2) for i in range(0, 16, 4)] + [(i, i - 2) for i in range(3, 16, 4)])
    x = jnp.where(jnp.where(even, li, nlat - 1 - li) % 4 == 2, got, x)
    x, kvw, kve, qo, qi, all_polar = lax.optimization_barrier((x, kvw, kve, qo, qi, all_polar))
    x2 = lax.ppermute(x, "lat", inner)

    o, st, ret_o, ret_i = call(
        window_kernel,
        (sds((PAIRS, 2, 128, LANES), F32), sds((2, 128, LANES)),
         sds((PAIRS + 1, 128, LANES)), sds((PAIRS + 1, 128, LANES))),
        [SMEM, SMEM, SMEM] + [VMEM] * 9,
        1000, 1000,
        [pltpu.VMEM((384, 384), F32), pltpu.VMEM((384, 384), F32)],
    )(band, table, widths, qo, qx, qy, qi, kv, kvw, kve, x, x2)
    ret_x = lax.ppermute(ret_o, "lat", outer)
    ret_y = lax.ppermute(ret_i, "lat", inner)

    far = lax.ppermute(all_polar[:, 128:], "lon", [(i, i ^ 8) for i in range(nlon)])
    all_polar, st = lax.optimization_barrier((all_polar, st))
    scratch = [pltpu.VMEM((1024, 2 * LANES), BF16), pltpu.VMEM((1024, LANES), BF16),
               pltpu.VMEM((1024, LANES), F32), pltpu.VMEM((1024, LANES), F32)]
    part = call(
        polar_near_kernel, sds((8, 80, LANES)), [SMEM, SMEM, SMEM, VMEM], 5_000_000_000, 1_000_000, scratch
    )(band, sector, table, all_polar)
    part = call(
        polar_far_kernel, sds((16, 80, LANES)), [SMEM, SMEM, SMEM, VMEM, VMEM, VMEM],
        3_000_000_000, 1_000_000, scratch,
    )(band, sector, table, all_polar, far, part)
    part = lax.all_to_all(part, "lon", 0, 0)

    part, ret_x, ret_y = lax.optimization_barrier((part, ret_x, ret_y))
    part2 = lax.ppermute(part, "lat", inner)

    out = call(
        merge_kernel, sds((2, 128, 512)), [SMEM] + [VMEM] * 5,
        1_000_000_000, 3_000_000, [pltpu.VMEM((256, 512), BF16)],
    )(band, o, st, ret_x, ret_y, wo)
    return pl.pallas_call(
        polar_row_kernel,
        out_shape=sds((2, 128, 512)),
        in_specs=[SMEM] + [VMEM] * 5 + [pl.BlockSpec(memory_space=pl.ANY)],
        out_specs=pl.BlockSpec(memory_space=pl.ANY),
        scratch_shapes=[pltpu.VMEM((128, 512), BF16), pltpu.VMEM((128, 512), BF16), pltpu.SemaphoreType.DMA],
        input_output_aliases={6: 0},
        compiler_params=PARAMS,
        cost_estimate=cost(1_000_000, 1_000_000),
    )(band, o, st, part, part2, wo, out)


def solution(mesh):
    in_specs = (P("lat", "lon", None), P(), P(), P(), P())
    return jax.shard_map(body, mesh=mesh, in_specs=in_specs, out_specs=P("lat", "lon", None), check_vma=False)
```

```python
import jax
import jax.numpy as jnp
import numpy as np
from jax import lax
from jax.experimental import pallas as pl
from jax.experimental.pallas import tpu as pltpu
from jax.sharding import PartitionSpec as P

HEADS = 8
HDIM = 64
NLAT = 32
PAIRS = 4
LANES = 128
MASKED = -1e30
F32 = jnp.float32
BF16 = jnp.bfloat16
VMEM = pl.BlockSpec(memory_space=pltpu.VMEM)
SMEM = pl.BlockSpec(memory_space=pltpu.SMEM)
PARAMS = pltpu.CompilerParams(vmem_limit_bytes=20 * 1024 * 1024)


def cost(flops, nbytes):
    return pl.CostEstimate(flops=flops, bytes_accessed=nbytes, transcendentals=0)


def row_tables():
    weight = lambda row: np.sin(np.pi * (row + 0.5) / NLAT) if 0 <= row < NLAT else 0.0
    table = np.zeros((NLAT // 2, 8), np.float32)
    for band in range(NLAT // 2):
        step = 1 - 2 * (band % 2)
        w = [weight(2 * band + band % 2 + step * k) for k in (-1, 0, 1, 2)]
        table[band, :4] = w[0] / (w[0] + w[2]), w[2] / (w[0] + w[2]), w[1] / (w[1] + w[3]), w[3] / (w[1] + w[3])
        table[band, 4:6] = np.log(w[1]), np.log(w[2])
        table[band, 6] = np.log(weight(0 if band in (0, NLAT // 2 - 1) else 1))
    return table.reshape(-1)


def is_polar(band):
    return (band == 0) | (band == NLAT // 2 - 1)


def lane_ids(shape):
    return lax.broadcasted_iota(jnp.int32, shape, len(shape) - 1)


def dot_nn(a, b):
    return lax.dot_general(a, b, (((1,), (0,)), ((), ())), preferred_element_type=F32)


def dot_nt(a, b):
    return lax.dot_general(a, b, (((1,), (1,)), ((), ())), preferred_element_type=F32)


def dot_tn(a, b):
    return lax.dot_general(a, b, (((0,), (0,)), ((), ())), preferred_element_type=F32)


def half_turn(x):
    return pltpu.roll(x, HDIM, 1)


def three_parts(x):
    a = x.astype(BF16)
    rest = x - a.astype(F32)
    b = rest.astype(BF16)
    c = (rest - b.astype(F32)).astype(BF16)
    return a.astype(F32), b.astype(F32), c.astype(F32)


def edge_kernel(band_ref, f_ref, fx_ref, fy_ref, last_ref, lead_ref):
    odd = band_ref[0] % 2
    for slot, out_ref in ((0, fx_ref), (1, fy_ref)):
        f = f_ref[odd if slot == 0 else 1 - odd]
        out_ref[...] = f
        last_ref[slot] = f[112:]
        lead_ref[slot] = f[:16]


def early_kernel(fx_ref, fy_ref, wq_ref, w_ref, qx_ref, qy_ref, pq_ref, base_ref):
    low = lane_ids((64, LANES)) < HDIM
    f = jnp.concatenate([fx_ref[...], fy_ref[...]], axis=0)
    q = dot_nn(f, wq_ref[...]).astype(BF16).astype(F32) * HDIM ** -0.5
    for p in range(PAIRS):
        block = q[:, p * LANES : (p + 1) * LANES]
        qx_ref[p] = block[:128].astype(BF16)
        qy_ref[p] = block[128:].astype(BF16)
        top, bottom = block[:64], block[64:128]
        pq_ref[2 * p] = jnp.where(low, top, half_turn(bottom)).astype(BF16)
        pq_ref[2 * p + 1] = jnp.where(low, half_turn(top), bottom).astype(BF16)
    base_ref[...] = dot_nn(f, w_ref[:512])


def keyval_kernel(
    band_ref, table_ref, fx_ref, fy_ref, outer_ref, inner_ref, west_ref, east_ref, pq_ref, base_ref, w_ref,
    kv_ref, kvx_ref, mine_ref, swap_ref,
):
    band = band_ref[0]
    coef = [table_ref[8 * band + i] for i in range(4)]
    for ref in (mine_ref, swap_ref):
        ref[:, 128:] = pq_ref[...]
    rows = [ref[...].astype(F32) for ref in (outer_ref, fx_ref, fy_ref, inner_ref)]
    cell = lax.broadcasted_iota(jnp.int32, (128, 512), 0)
    lat, lon = [], []
    for r in range(2):
        lat.append((coef[2 * r] * rows[r] + coef[2 * r + 1] * rows[r + 2]).astype(BF16))
        mid = rows[r + 1]
        before = jnp.where(cell == 0, west_ref[r, 15:16].astype(F32), pltpu.roll(mid, 1, 0))
        after = jnp.where(cell == 127, east_ref[r, 0:1].astype(F32), pltpu.roll(mid, 127, 0))
        lon.append((0.5 * (before + after)).astype(BF16))
    basis = [jnp.concatenate(x, axis=0) for x in (lat, lon)]
    low = lane_ids((256, LANES)) < HDIM
    for p in range(PAIRS):
        parts = []
        for side in range(2):
            c = slice(512 * side + p * LANES, 512 * side + (p + 1) * LANES)
            parts.append(
                base_ref[:, c] + dot_nn(basis[0], w_ref[512:1024, c]) + dot_nn(basis[1], w_ref[1024:, c])
            )
        k, v = parts
        v = half_turn(v)
        for h, packed in ((2 * p, jnp.where(low, k, v)), (2 * p + 1, jnp.where(low, v, k))):
            packed = packed.astype(BF16)
            kv_ref[0, h] = packed[:128]
            kv_ref[1, h] = packed[128:]
            kvx_ref[h] = packed[:128]
            mine_ref[h, :128] = packed[:128]
            swap_ref[h, :128] = packed[128:]


def pick_kernel(band_ref, own_ref, got_ref, out_ref):
    @pl.when(is_polar(band_ref[0]))
    def _():
        out_ref[...] = own_ref[...]

    @pl.when((band_ref[0] == 1) | (band_ref[0] == NLAT // 2 - 2))
    def _():
        out_ref[...] = got_ref[...]


def window_kernel(
    band_ref, table_ref, width_ref, qo_ref, qx_ref, qy_ref, qi_ref, kv_ref, kvw_ref, kve_ref, p1_ref, p2_ref,
    o_ref, st_ref, ro_ref, ri_ref, bias_x, bias_y,
):
    ahead = lax.broadcasted_iota(jnp.int32, (128, 384), 1) - 128
    here = lax.broadcasted_iota(jnp.int32, (128, 384), 0)
    gap = jnp.abs(ahead - here)
    band = band_ref[0]
    first = 2 * band + band % 2
    step = 1 - 2 * (band % 2)
    for t in range(4):
        row = first + step * (t - 1)
        inner_row = (row > 0) & (row < NLAT - 1)
        inside = gap <= jnp.where(inner_row, width_ref[jnp.clip(row, 0, NLAT - 1)], -1)
        if t < 3:
            bias_x[t * 128 : (t + 1) * 128] = jnp.where(inside, table_ref[8 * band + 4], MASKED)
        if t > 0:
            bias_y[(t - 1) * 128 : t * 128] = jnp.where(inside, table_ref[8 * band + 5], MASKED)
    lane = lane_ids((128, LANES))
    low = lane < HDIM
    ones = jnp.ones((384, LANES), BF16)
    stats = [jnp.zeros((128, LANES), F32) for _ in range(4)]
    for p in range(PAIRS):
        halves = []
        for odd in range(2):
            h = 2 * p + odd
            keep = (lane >= HDIM) if odd else low
            qs = [qo_ref[p], qx_ref[p], qy_ref[p], qi_ref[p]]
            qs = [jnp.where(keep, x, jnp.zeros_like(x)) for x in qs]
            kva = jnp.concatenate([kvw_ref[0, h], kv_ref[0, h], kve_ref[0, h]], axis=0)
            kvb = jnp.concatenate([kvw_ref[1, h], kv_ref[1, h], kve_ref[1, h]], axis=0)
            kvp = jnp.concatenate([p1_ref[h], p2_ref[h]], axis=0)
            sa = dot_nt(jnp.concatenate(qs[:3], axis=0), kva) + bias_x[...]
            sb = dot_nt(jnp.concatenate(qs[1:], axis=0), kvb) + bias_y[...]
            sp = dot_nt(jnp.concatenate(qs[1:3], axis=0), kvp)
            ma = jnp.max(sa, axis=1, keepdims=True)
            mb = jnp.max(sb, axis=1, keepdims=True)
            mp = jnp.max(sp, axis=1, keepdims=True)
            mid = jnp.maximum(jnp.maximum(ma[128:], mb[:256]), mp)
            mo = ma[:128]
            mi = mb[256:]
            pa = jnp.exp(sa - jnp.concatenate([mo, mid], axis=0)).astype(BF16)
            pb = jnp.exp(sb - jnp.concatenate([mid, mi], axis=0)).astype(BF16)
            pp = jnp.exp(sp - mid).astype(BF16)
            oa = dot_nn(pa, jnp.concatenate([kva, ones], axis=1))
            ob = dot_nn(pb, jnp.concatenate([kvb, ones], axis=1))
            op = dot_nn(pp, jnp.concatenate([kvp, ones[:256]], axis=1))
            om = oa[128:] + ob[:256] + op
            full = [oa[:128], om[:128], om[128:], ob[256:]]
            tops = [mo, mid[:128], mid[128:], mi]
            halves.append([x[:, :LANES] / x[:, LANES:] for x in full])
            for t in range(4):
                parts = three_parts(tops[t] + jnp.log(full[t][:, LANES:]))
                for i in range(3):
                    stats[t] = jnp.where(lane == 3 * h + i, parts[i], stats[t])
        both = [jnp.where(low, halves[1][t], halves[0][t]) for t in range(4)]
        ro_ref[p] = both[0].astype(BF16)
        o_ref[p, 0] = both[1]
        o_ref[p, 1] = both[2]
        ri_ref[p] = both[3].astype(BF16)
    ro_ref[PAIRS] = stats[0].astype(BF16)
    st_ref[0] = stats[1].astype(BF16)
    st_ref[1] = stats[2].astype(BF16)
    ri_ref[PAIRS] = stats[3].astype(BF16)


def polar_near_kernel(band_ref, sector_ref, table_ref, in_ref, out_ref, wide, q_all, o_all, l_all):
    @pl.when((band_ref[0] < 2) | (band_ref[0] >= NLAT // 2 - 2))
    def _():
        queries = [in_ref[b, 128:] for b in range(8)]
        polar_part(band_ref, sector_ref, table_ref, in_ref, queries, out_ref, 0, wide, q_all, o_all, l_all)


def polar_far_kernel(band_ref, sector_ref, table_ref, in_ref, far_ref, part_ref, out_ref, wide, q_all, o_all, l_all):
    @pl.when((band_ref[0] < 2) | (band_ref[0] >= NLAT // 2 - 2))
    def _():
        near = 8 * (sector_ref[0] // 8)
        queries = [far_ref[b] for b in range(8)]
        polar_part(band_ref, sector_ref, table_ref, in_ref, queries, out_ref, 8 - near, wide, q_all, o_all, l_all)
        for b in range(8):
            out_ref[near + b] = part_ref[b]


def polar_part(band_ref, sector_ref, table_ref, in_ref, queries, out_ref, base, wide, q_all, o_all, l_all):
    odd = sector_ref[0] % 2
    log = table_ref[8 * band_ref[0] + 6]
    lane = lane_ids((128, LANES))
    keep = (lane // HDIM) == odd
    low = lane_ids((64, LANES)) < HDIM
    for b in range(8):
        wide[128 * b : 128 * (b + 1), :LANES] = in_ref[b, :128]
    wide[:, LANES:] = jnp.ones((1024, LANES), BF16)
    for b in range(8):
        packed = queries[b].astype(F32)
        turned = half_turn(packed)
        first = jnp.where(odd == 1, turned, packed)
        second = jnp.where(odd == 1, packed, turned)
        q = jnp.where(keep, jnp.concatenate([first, second], axis=0), 0.0)
        q_all[128 * b : 128 * (b + 1)] = q.astype(BF16)

    for b in range(4):
        rows = slice(256 * b, 256 * (b + 1))
        s = dot_nt(q_all[rows], wide[:, :LANES])
        m = jnp.max(s, axis=1, keepdims=True)
        e = jnp.exp(s - m).astype(BF16)
        full = dot_nn(e, wide[...])
        total = full[:, LANES:]
        o_all[rows] = full[:, :LANES] / total
        l_all[rows] = m + jnp.log(total) + log

    pick = jnp.where(
        lax.broadcasted_iota(jnp.int32, (16, LANES), 0) == lane_ids((16, LANES)), 1.0, 0.0
    ).astype(BF16)
    for b in range(8):
        out = o_all[128 * b : 128 * (b + 1)]
        turned = half_turn(out)
        left = jnp.where(odd == 1, out[:64], turned[:64])
        right = jnp.where(odd == 1, turned[64:], out[64:])
        out_ref[base + b, :64] = jnp.where(low, left, right).astype(BF16)
        parts = three_parts(l_all[128 * b : 128 * (b + 1)])
        stats = jnp.zeros((128, LANES), F32)
        for i in range(3):
            stats = jnp.where(lane == i, parts[i], stats)
        out_ref[base + b, 64:] = dot_nt(pick, stats.astype(BF16)).astype(BF16)


def head_pick():
    src = lax.broadcasted_iota(jnp.int32, (LANES, 512), 0) // 3
    dst = lax.broadcasted_iota(jnp.int32, (LANES, 512), 1)
    head = 2 * (dst // LANES) + jnp.where(dst % LANES < HDIM, 1, 0)
    return jnp.where(src == head, 1.0, 0.0).astype(BF16)


def turned_weights(wo_ref):
    order = []
    for p in range(PAIRS):
        order += [wo_ref[p * LANES + HDIM : (p + 1) * LANES], wo_ref[p * LANES : p * LANES + HDIM]]
    return jnp.concatenate(order, axis=0)


def merge_kernel(band_ref, o_ref, st_ref, rx_ref, ry_ref, wo_ref, out_ref, att):
    odd = band_ref[0] % 2
    pick = head_pick()
    for r, ret in ((0, rx_ref), (1, ry_ref)):
        lse = dot_nn(st_ref[r], pick)
        lse_ret = dot_nn(ret[PAIRS], pick)
        mine = jnp.concatenate([o_ref[p, r] for p in range(PAIRS)], axis=1)
        other = jnp.concatenate([ret[p] for p in range(PAIRS)], axis=1).astype(F32)
        top = jnp.maximum(lse, lse_ret)
        wa = jnp.exp(lse - top)
        wb = jnp.exp(lse_ret - top)
        att[r * 128 : (r + 1) * 128] = ((mine * wa + other * wb) / (wa + wb)).astype(BF16)
    out = dot_nn(att[...], turned_weights(wo_ref)).astype(BF16)
    out_ref[odd] = out[:128]
    out_ref[1 - odd] = out[128:]


def polar_row_kernel(band_ref, o_ref, st_ref, p1_ref, p2_ref, wo_ref, old_ref, out_ref, att, row_ref, sem):
    odd = band_ref[0] % 2

    @pl.when(is_polar(band_ref[0]))
    def _():
        lse = dot_nn(st_ref[0], head_pick())
        low = lane_ids((64, LANES)) < HDIM
        row = lax.broadcasted_iota(jnp.int32, (16, LANES), 0)
        col = lane_ids((16, LANES))
        pick_even = jnp.where((row < 3) & (col >= HDIM), 1.0, 0.0).astype(BF16)
        pick_odd = jnp.where((row < 3) & (col < HDIM), 1.0, 0.0).astype(BF16)
        for p in range(PAIRS):
            vals, logs = [o_ref[p, 0]], [lse[:, p * LANES : (p + 1) * LANES]]
            for ref, h in ((p1_ref, 2 * p), (p1_ref, 8 + 2 * p), (p2_ref, 2 * p), (p2_ref, 8 + 2 * p)):
                even32, odd32 = ref[h, :64].astype(F32), ref[h + 1, :64].astype(F32)
                first = jnp.where(low, odd32, half_turn(even32))
                second = jnp.where(low, half_turn(odd32), even32)
                vals.append(jnp.concatenate([first, second], axis=0))
                logs.append(dot_tn(ref[h, 64:], pick_even) + dot_tn(ref[h + 1, 64:], pick_odd))
            best = logs[0]
            for x in logs[1:]:
                best = jnp.maximum(best, x)
            scales = [jnp.exp(x - best) for x in logs]
            merged = sum(v * w for v, w in zip(vals, scales)) / sum(scales)
            att[:, p * LANES : (p + 1) * LANES] = merged.astype(BF16)
        row_ref[...] = dot_nn(att[...], turned_weights(wo_ref)).astype(BF16)
        copy = pltpu.make_async_copy(row_ref, out_ref.at[odd], sem)
        copy.start()
        copy.wait()


def call(kernel, outs, in_specs, flops, nbytes, scratch=(), out_specs=None):
    return pl.pallas_call(
        kernel,
        out_shape=outs,
        grid=(1,),
        in_specs=in_specs,
        out_specs=out_specs or jax.tree.map(lambda _: VMEM, outs),
        scratch_shapes=list(scratch),
        compiler_params=PARAMS,
        cost_estimate=cost(flops, nbytes),
    )


def sds(shape, dtype=BF16):
    return jax.ShapeDtypeStruct(shape, dtype)


def ring(n, k):
    return [(i, (i + k) % n) for i in range(n)]


def body(gf, widths, wq, wkv, wo):
    nlat, nlon = NLAT // 2, 16
    li = lax.axis_index("lat").astype(jnp.int32)
    lj = lax.axis_index("lon").astype(jnp.int32)
    band, sector = li.reshape(1), lj.reshape(1)
    table = jnp.asarray(row_tables())
    inner = [(i, i ^ 1) for i in range(nlat)]
    outer = [(i, i + 1 if i % 2 else i - 1) for i in range(1, nlat - 1)]
    groups = [list(range(8)), list(range(8, 16))]

    fx, fy, last, lead = call(
        edge_kernel,
        (sds((128, 512)), sds((128, 512)), sds((2, 16, 512)), sds((2, 16, 512))),
        [SMEM, VMEM], 8_000_000_000, 100_000,
    )(band, gf)
    over = lax.ppermute(fx, "lat", outer)
    beside = lax.ppermute(fy, "lat", inner)
    west = lax.ppermute(last, "lon", ring(nlon, 1))
    east = lax.ppermute(lead, "lon", ring(nlon, -1))
    qx, qy, pq, base = call(
        early_kernel,
        (sds((PAIRS, 128, LANES)), sds((PAIRS, 128, LANES)), sds((HEADS, 64, LANES)), sds((256, 1024), F32)),
        [VMEM] * 4,
        600_000_000, 6_000_000,
    )(fx, fy, wq, wkv)

    kv, kvx, mine, swap = call(
        keyval_kernel,
        (sds((2, HEADS, 128, LANES)), sds((HEADS, 128, LANES)),
         sds((HEADS, 192, LANES)), sds((HEADS, 192, LANES))),
        [SMEM, SMEM] + [VMEM] * 9,
        1_000_000_000, 4_000_000,
    )(band, table, fx, fy, over, beside, west, east, pq, base, wkv)

    got = lax.ppermute(swap, "lat", inner)
    picked = call(pick_kernel, sds((HEADS, 192, LANES)), [SMEM] + [VMEM] * 2, 1000, 1_000_000)(
        band, mine, got
    )
    all_polar = lax.all_to_all(picked, "lon", 0, 0, axis_index_groups=groups)

    kvx, kv_later, picked = lax.optimization_barrier((kvx, kv, picked))
    kvw = lax.ppermute(kv_later, "lon", ring(nlon, 1))
    kve = lax.ppermute(kv_later, "lon", ring(nlon, -1))
    qo = lax.ppermute(qx, "lat", outer)
    qi = lax.ppermute(qy, "lat", inner)

    even = li % 2 == 0
    x = kvx
    for step in (4, 8, 12):
        got = lax.ppermute(kvx, "lat", [(0, step), (nlat - 1, nlat - 1 - step)])
        x = jnp.where(jnp.where(even, li, nlat - 1 - li) == step, got, x)
    got = lax.ppermute(x, "lat", [(i, i + 2) for i in range(0, 16, 4)] + [(i, i - 2) for i in range(3, 16, 4)])
    x = jnp.where(jnp.where(even, li, nlat - 1 - li) % 4 == 2, got, x)
    x, kvw, kve, qo, qi, all_polar = lax.optimization_barrier((x, kvw, kve, qo, qi, all_polar))
    x2 = lax.ppermute(x, "lat", inner)

    o, st, ret_o, ret_i = call(
        window_kernel,
        (sds((PAIRS, 2, 128, LANES), F32), sds((2, 128, LANES)),
         sds((PAIRS + 1, 128, LANES)), sds((PAIRS + 1, 128, LANES))),
        [SMEM, SMEM, SMEM] + [VMEM] * 9,
        1000, 1000,
        [pltpu.VMEM((384, 384), F32), pltpu.VMEM((384, 384), F32)],
    )(band, table, widths, qo, qx, qy, qi, kv, kvw, kve, x, x2)
    ret_x = lax.ppermute(ret_o, "lat", outer)
    ret_y = lax.ppermute(ret_i, "lat", inner)

    far = lax.ppermute(all_polar[:, 128:], "lon", [(i, i ^ 8) for i in range(nlon)])
    all_polar, st = lax.optimization_barrier((all_polar, st))
    scratch = [pltpu.VMEM((1024, 2 * LANES), BF16), pltpu.VMEM((1024, LANES), BF16),
               pltpu.VMEM((1024, LANES), F32), pltpu.VMEM((1024, LANES), F32)]
    part = call(
        polar_near_kernel, sds((8, 80, LANES)), [SMEM, SMEM, SMEM, VMEM], 5_000_000_000, 1_000_000, scratch
    )(band, sector, table, all_polar)
    part = call(
        polar_far_kernel, sds((16, 80, LANES)), [SMEM, SMEM, SMEM, VMEM, VMEM, VMEM],
        3_000_000_000, 1_000_000, scratch,
    )(band, sector, table, all_polar, far, part)
    part = lax.all_to_all(part, "lon", 0, 0)

    part, ret_x, ret_y = lax.optimization_barrier((part, ret_x, ret_y))
    part2 = lax.ppermute(part, "lat", inner)

    out = call(
        merge_kernel, sds((2, 128, 512)), [SMEM] + [VMEM] * 5,
        1_000_000_000, 3_000_000, [pltpu.VMEM((256, 512), BF16)],
    )(band, o, st, ret_x, ret_y, wo)
    return pl.pallas_call(
        polar_row_kernel,
        out_shape=sds((2, 128, 512)),
        in_specs=[SMEM] + [VMEM] * 5 + [pl.BlockSpec(memory_space=pl.ANY)],
        out_specs=pl.BlockSpec(memory_space=pl.ANY),
        scratch_shapes=[pltpu.VMEM((128, 512), BF16), pltpu.VMEM((128, 512), BF16), pltpu.SemaphoreType.DMA],
        input_output_aliases={6: 0},
        compiler_params=PARAMS,
        cost_estimate=cost(1_000_000, 1_000_000),
    )(band, o, st, part, part2, wo, out)


def solution(mesh):
    in_specs = (P("lat", "lon", None), P(), P(), P(), P())
    return jax.shard_map(body, mesh=mesh, in_specs=in_specs, out_specs=P("lat", "lon", None), check_vma=False)
```
